1024 devices in a mesh: dp: 64 (over z, core), expert: 16 (over x, y).
Axes of the slice: x: 4, y: 4, z: 32, core: 2. Of those that a mesh axis runs over, the one named last changes fastest.
Arguments:
- tokens: bfloat16 [16384, 2048], P(('dp', 'expert')), may hold values from -6 to 6
- grad_out: bfloat16 [16384, 2048], P(('dp', 'expert')), may hold values from -6 to 6
- gate_probs: bfloat16 [16384, 8], P(('dp', 'expert')), may hold values from 0.049804688 to 1
- routes: int32 [16384, 8], P(('dp', 'expert')), may hold values from 0 to 15, as said below
- capacity: int32 [64, 16], P('dp', 'expert'), may hold values from 64 to 128, as said below
- pair_mask: int32 [16], P('expert'), may hold values from 1 to 32, as said below
- gate_up_weight: bfloat16 [16, 2048, 1536], P('expert'), may hold values from -0.125 to 0.125
- down_weight: bfloat16 [16, 2048, 768], P('expert'), may hold values from -0.21875 to 0.21875
Outputs:
- layer_out: bfloat16 [16384, 2048], P(('dp', 'expert'))
- input_grad: bfloat16 [16384, 2048], P(('dp', 'expert'))
- gate_grad: float32 [16384, 8], P(('dp', 'expert'))
The draws below stay inside these ranges and needn't reach their ends.
Inputs may be any that keep to these rules, and one draw needn't show every extreme that they name: `routes`: each token names 8 different experts. The tokens of one device name any one expert at most 12 times; one expert, the same for all devices, is named exactly 12 times by the tokens of every device. `capacity`: both ends of the range occur in every draw. `pair_mask`: each entry is a power of two; both ends of the range occur in every draw.
All inputs are finite; a program needn't handle non-finite values.
Results may differ from the reference program's by a relative error of at most 0.01.
Values may be sent and summed in bfloat16 or wider, within the bound.
A program may use at most 64 MiB of HBM per device.

```python
import math
import jax
import jax.numpy as jnp
from jax import lax

D = 2048
FFE = 768
TOPK = 8
EXPERTS = 16
TOK_DEV = 16
MOST = 12
CAP = 128
OVF = 16
TOKENS = 16384
N_DP = 64
N_EXPERT = 16


def hot_choice(key):
    return jax.random.randint(jax.random.fold_in(key, 11), (), 0, EXPERTS)


def draw_routes(key, part):
    blocks = TOKENS // TOK_DEV
    others = EXPERTS - 1
    hot_id = hot_choice(key)
    block_keys = jax.random.split(jax.random.fold_in(key, 12), blocks)

    def one_block(block_key):
        perm_key, start_key, label_key, rotate_key = jax.random.split(block_key, 4)
        hot_rank = jax.random.permutation(perm_key, TOK_DEV)
        start_rank = jax.random.permutation(start_key, TOK_DEV)
        relabel = jax.random.permutation(label_key, others)
        rotation = jax.random.randint(rotate_key, (), 0, others)
        has_hot = (hot_rank < MOST).astype(jnp.int32)
        window_start = start_rank * others // TOK_DEV + rotation
        column = jnp.arange(TOPK, dtype=jnp.int32)
        other_pos = (window_start[:, None] + column[None, :] - has_hot[:, None]) % others
        other_id = (hot_id + 1 + relabel[other_pos]) % EXPERTS
        chosen = jnp.where((has_hot[:, None] == 1) & (column[None, :] == 0), hot_id, other_id)
        return chosen.astype(jnp.int32)
    return jax.vmap(one_block)(block_keys).reshape(TOKENS, TOPK)


def draw_capacity(key, part):
    caps = jax.random.randint(jax.random.fold_in(key, 21), (N_DP, EXPERTS), CAP // 2, CAP + 1)
    hot_id = hot_choice(key)
    row_pick = jax.random.randint(jax.random.fold_in(key, 22), (), 0, N_DP)
    row_ids = jnp.arange(N_DP, dtype=jnp.int32)[:, None]
    col_ids = jnp.arange(EXPERTS, dtype=jnp.int32)[None, :]
    caps = jnp.where((row_ids == row_pick) & (col_ids == hot_id), CAP, caps)
    caps = jnp.where((row_ids == row_pick) & (col_ids == (hot_id + 1) % EXPERTS), CAP // 2, caps)
    return caps.astype(jnp.int32)


def draw_pair_mask(key, part):
    levels = N_DP.bit_length() - 1
    powers = jax.random.randint(jax.random.fold_in(key, 31), (EXPERTS,), 0, levels)
    first_pick = jax.random.randint(jax.random.fold_in(key, 32), (), 0, EXPERTS)
    second_pick = (first_pick + 1 + jax.random.randint(jax.random.fold_in(key, 33), (), 0, EXPERTS - 1)) % EXPERTS
    index_ids = jnp.arange(EXPERTS, dtype=jnp.int32)
    powers = jnp.where(index_ids == first_pick, 0, powers)
    powers = jnp.where(index_ids == second_pick, levels - 1, powers)
    return jnp.left_shift(jnp.ones((EXPERTS,), jnp.int32), powers.astype(jnp.int32))


def block_levels(own_key, dims, shards, low, top_value):
    def one(axis_at, blocks):
        draws = jax.random.uniform(jax.random.fold_in(jax.random.fold_in(own_key, 6), axis_at), (blocks,), jnp.float32, low / len(shards), top_value / len(shards))
        return jnp.repeat(jnp.exp(draws), dims[axis_at] // blocks).reshape((-1,) + (1,) * (len(dims) - axis_at - 1))

    level = one(*shards[0])
    for cut in shards[1:]:
        level = level * one(*cut)
    return level


def scatter_about(key, dims, spread, bound, pieces=(), kind=jnp.bfloat16):
    factor_of = block_levels(key, dims, pieces, -0.22, 0.18) if pieces else 1.0
    drawn = jax.random.normal(key, dims, jnp.float32) * spread * factor_of
    return jnp.minimum(jnp.maximum(drawn, -bound), bound).astype(kind)


def setup_inputs(seed: int = 0) -> dict:
    key_of = jax.random.split(jax.random.key(seed), 9)
    tokens = scatter_about(key_of[0], (TOKENS, D), 1.0, 6.0, ((0, 1024),))
    grad_out = scatter_about(key_of[1], (TOKENS, D), 1.0, 6.0, ((0, 1024),))
    gate_probs = jnp.clip(jnp.exp(math.log(1.0) - 2.9996462 * jax.random.uniform(key_of[2], (TOKENS, TOPK), jnp.float32) ** block_levels(key_of[2], (TOKENS, TOPK), ((0, 1024),), -0.2, 0.2)), 0.049804688, 1.0).astype(jnp.bfloat16)
    routes = draw_routes(jax.random.fold_in(key_of[8], 71), 0)
    capacity = draw_capacity(jax.random.fold_in(key_of[8], 71), 0)
    pair_mask = draw_pair_mask(jax.random.fold_in(key_of[8], 71), 0)
    gate_up_weight = scatter_about(key_of[6], (EXPERTS, D, 2 * FFE), D ** -0.5, 0.125, ((0, 16),))
    down_weight = scatter_about(key_of[7], (EXPERTS, D, FFE), FFE ** -0.5, 0.21875, ((0, 16),))
    return dict(tokens=tokens, grad_out=grad_out, gate_probs=gate_probs, routes=routes, capacity=capacity, pair_mask=pair_mask, gate_up_weight=gate_up_weight, down_weight=down_weight)


def pick_rows(table, index):
    return jnp.take(table, index, axis=0, mode="fill", fill_value=0)


def expert_rows(row_input, row_scaled, w_gate_up, w_down):
    hidden_units = w_down.shape[1]
    both = jnp.dot(row_input, w_gate_up, preferred_element_type=jnp.float32)
    gate_pre = both[:, :hidden_units]
    up_pre = both[:, hidden_units:]
    sigma = jax.nn.sigmoid(gate_pre)
    swish = gate_pre * sigma
    hidden = (swish * up_pre).astype(jnp.bfloat16)
    outputs = lax.dot_general(hidden, w_down, (((1,), (1,)), ((), ())), preferred_element_type=jnp.float32).astype(jnp.bfloat16)
    back_hidden = jnp.dot(row_scaled, w_down, preferred_element_type=jnp.float32)
    d_gate = back_hidden * up_pre * sigma * (1.0 + gate_pre * (1.0 - sigma))
    d_up = back_hidden * swish
    d_both = jnp.concatenate([d_gate, d_up], axis=1).astype(jnp.bfloat16)
    row_grads = lax.dot_general(d_both, w_gate_up, (((1,), (1,)), ((), ())), preferred_element_type=jnp.float32).astype(jnp.bfloat16)
    return outputs, row_grads


def reference(tokens, grad_out, gate_probs, routes, capacity, pair_mask, gate_up_weight, down_weight):
    per_row = TOK_DEV * N_EXPERT
    route_count = per_row * TOPK
    span = CAP + OVF
    row_routes = routes.reshape(N_DP, route_count)
    expert_ids = jnp.arange(EXPERTS, dtype=jnp.int32)
    queue_length = jnp.sum((row_routes[:, :, None] == expert_ids[None, None, :]).astype(jnp.int32), axis=1)
    home_rows = jnp.minimum(queue_length, capacity)
    spare_rows = capacity - home_rows
    partner = jnp.bitwise_xor(jnp.arange(N_DP, dtype=jnp.int32)[:, None], pair_mask[None, :])
    partner_spare = jnp.take_along_axis(spare_rows, partner, axis=0)
    keep_limit = capacity + jnp.minimum(partner_spare, OVF)

    def one_row(packed):
        row_tokens, row_grad, row_gates, row_route, row_limit = packed
        flat_gates = row_gates.reshape(route_count).astype(jnp.float32)

        def one_expert(carry, expert_id):
            out_sum, grad_sum, gate_sum = carry
            route_hit = (row_route == expert_id).astype(jnp.int32)
            queue_pos = jnp.cumsum(route_hit) - 1
            target = jnp.where((route_hit == 1) & (queue_pos < span), queue_pos, span)
            source = jnp.full((span + 1,), route_count, jnp.int32).at[target].set(jnp.arange(route_count, dtype=jnp.int32))[:span]
            kept_row = (source < route_count) & (jnp.arange(span, dtype=jnp.int32) < row_limit[expert_id])
            token_index = jnp.where(kept_row, source // TOPK, per_row).astype(jnp.int32)
            route_index = jnp.where(kept_row, source, route_count).astype(jnp.int32)
            row_input = pick_rows(row_tokens, token_index)
            rows_grad = pick_rows(row_grad, token_index)
            rows_gate = jnp.take(flat_gates, route_index, mode="fill", fill_value=0.0)
            row_scaled = (rows_gate[:, None] * rows_grad.astype(jnp.float32)).astype(jnp.bfloat16)
            outputs, row_grads = expert_rows(row_input, row_scaled, gate_up_weight[expert_id], down_weight[expert_id])
            out_float = outputs.astype(jnp.float32)
            out_sum = out_sum.at[token_index].add(rows_gate[:, None] * out_float, mode="drop")
            grad_sum = grad_sum.at[token_index].add(row_grads.astype(jnp.float32), mode="drop")
            gate_sum = gate_sum.at[route_index].add(jnp.sum(rows_grad.astype(jnp.float32) * out_float, axis=1), mode="drop")
            return (out_sum, grad_sum, gate_sum), None

        initial = (jnp.zeros((per_row, D), jnp.float32), jnp.zeros((per_row, D), jnp.float32), jnp.zeros((route_count,), jnp.float32))
        scan_result = lax.scan(one_expert, initial, expert_ids)
        out_sum, grad_sum, gate_sum = scan_result[0]
        return out_sum.astype(jnp.bfloat16), grad_sum.astype(jnp.bfloat16), gate_sum.reshape(per_row, TOPK)

    results = lax.map(one_row, (tokens.reshape(N_DP, per_row, D), grad_out.reshape(N_DP, per_row, D), gate_probs.reshape(N_DP, per_row, TOPK), row_routes, keep_limit))
    return (results[0].reshape(TOKENS, D), results[1].reshape(TOKENS, D), results[2].reshape(TOKENS, TOPK))
```

```python
import functools

import jax
import jax.numpy as jnp
from jax import lax
from jax.experimental import pallas as pl
from jax.experimental.pallas import tpu as pltpu
from jax.sharding import PartitionSpec as P

TOPK = 8
OVF = 16
MEMBERS = 16
TOK = 16
PARTS = 4
ROWS = MEMBERS * TOK
HALF = ROWS // 2
TILE = 256
CHUNK = 32
LANES = 128
MESH = pl.DeviceIdType.MESH

ORDER = [[(q + s) % 4 for s in range(4)] for q in range(PARTS)]


def slot_of(q, p):
    return sum(1 << ORDER[q][s] for s in range(4) if p >> s & 1)


PLACE = [{slot_of(q, p): p for p in range(MEMBERS)} for q in range(PARTS)]
SLOT = [[slot_of(q, p) for p in range(MEMBERS)] for q in range(PARTS)]
STEP_AT = [0, 128, 192, 224]
STEP_ROWS = [128, 64, 32, 16]


def flip(v, bits):
    if bits & 2:
        v = 3 - v
    if bits & 1:
        v = v + 1 - 2 * lax.rem(v, 2)
    return v


def recode(v):
    return v ^ ((v >> 1) & 5)


def nt_dot(a, b):
    return lax.dot_general(a, b, (((1,), (1,)), ((), ())), preferred_element_type=jnp.float32)


def nn_dot(a, b):
    return jnp.dot(a, b, preferred_element_type=jnp.float32)


def kernel(
    levels,
    tokens,
    grads,
    gates,
    routes,
    capacity,
    pair_mask,
    gate_up,
    down,
    out_ref,
    igrad_ref,
    ggrad_ref,
    gu_v,
    dn_v,
    xb,
    sb,
    rb,
    acc,
    p1,
    p2,
    p3,
    hid,
    dpre,
    ta,
    tb,
    gsend,
    grecv,
    gmat,
    gkeep,
    gcol,
    ggacc,
    qsend,
    qrecv,
    dsend,
    drecv,
    local_sem,
    weight_sem,
    ag_send,
    ag_recv,
    rs_send,
    rs_recv,
    g_send,
    g_recv,
    q_send,
    q_recv,
    d_send,
    d_recv,
):
    width = tokens.shape[1]
    part = width // PARTS
    hidden = down.shape[2]
    dp = lax.axis_index("dp")
    me = lax.axis_index("expert")
    mx, my = lax.div(me, 4), lax.rem(me, 4)

    def member(j):
        return (dp, flip(mx, j >> 2) * 4 + flip(my, j & 3))

    def partner(b):
        step = 1 << b
        return (dp + step * (1 - 2 * lax.rem(lax.div(dp, step), 2)), me)

    barrier = pltpu.get_barrier_semaphore()
    everyone = [member(j) for j in range(1, MEMBERS)] + [partner(b) for b in range(levels)]
    for other in everyone:
        pl.semaphore_signal(barrier, inc=1, device_id=other, device_id_type=MESH)

    sources = (tokens, grads)
    local = []
    for a in range(2):
        for q in range(PARTS):
            copy = pltpu.make_async_copy(
                sources[a].at[:, q * part : (q + 1) * part],
                xb.at[a * PARTS + q, 0:TOK, :],
                local_sem.at[a * PARTS + q],
            )
            copy.start()
            local.append(copy)
    weights = []
    for i in range(PARTS):
        rows = slice(i * part, (i + 1) * part)
        weights.append(
            pltpu.make_async_copy(gate_up.at[0, rows, :], gu_v.at[rows, :], weight_sem.at[i])
        )
    for i in range(PARTS):
        rows = slice(i * part, (i + 1) * part)
        weights.append(
            pltpu.make_async_copy(down.at[0, rows, :], dn_v.at[rows, :], weight_sem.at[4 + i])
        )
    for copy in weights:
        copy.start()

    my_code = recode(me)
    rel = recode(routes[...]) ^ my_code
    lane = lax.broadcasted_iota(jnp.int32, (TOK, LANES), 1)
    sub = lax.broadcasted_iota(jnp.int32, (TOK, LANES), 0)
    gate_values = gates[...].astype(jnp.float32)
    dense = jnp.zeros((TOK, LANES), jnp.float32)
    for k in range(TOPK):
        dense += jnp.where(lane == rel[:, k : k + 1], gate_values[:, k : k + 1], 0.0)
    square = jnp.concatenate([dense, jnp.zeros((LANES - TOK, LANES), jnp.float32)], axis=0)
    turned = square.T
    for j in range(MEMBERS):
        gsend[j] = turned[j : j + 1, :]

    pl.semaphore_wait(barrier, len(everyone))

    def gather(a, q, s):
        n = a * PARTS + q
        held = TOK << s
        if s == 0:
            src = sources[a].at[:, q * part : (q + 1) * part]
        else:
            src = xb.at[n, 0:held, :]
        return pltpu.make_async_remote_copy(
            src_ref=src,
            dst_ref=xb.at[n, held : 2 * held, :],
            send_sem=ag_send.at[n * 4 + s],
            recv_sem=ag_recv.at[n * 4 + s],
            device_id=member(1 << ORDER[q][s]),
            device_id_type=MESH,
        )

    def small(src, dst, send, recv, index, slot, other):
        return pltpu.make_async_remote_copy(
            src_ref=src.at[index],
            dst_ref=dst.at[slot],
            send_sem=send.at[slot],
            recv_sem=recv.at[slot],
            device_id=other,
            device_id_type=MESH,
        )

    gates_to = [small(gsend, grecv, g_send, g_recv, j, j, member(j)) for j in range(1, MEMBERS)]
    spare_to = [small(dsend, drecv, d_send, d_recv, 0, b, partner(b)) for b in range(levels)]
    quot_to = [small(qsend, qrecv, q_send, q_recv, j, j, member(j)) for j in range(1, MEMBERS)]

    for a in range(2):
        for q in range(PARTS):
            gather(a, q, 0).start()
    for copy in gates_to:
        copy.start()
    for copy in local:
        copy.wait()
    for s in range(1, 4):
        for a in range(2):
            if (a, s) == (1, 3):
                break
            for q in range(PARTS):
                gather(a, q, s - 1).wait_recv()
                gather(a, q, s).start()

    gmat[0:1, :] = gsend[0]
    for j in range(1, MEMBERS):
        gates_to[j - 1].wait_recv()
        gmat[j : j + 1, :] = grecv[j]
    mat = gmat[...]
    named = jnp.where(mat > 0.0, 1.0, 0.0)
    named16 = named.astype(jnp.bfloat16)
    big0 = lax.broadcasted_iota(jnp.int32, (LANES, LANES), 0)
    big1 = lax.broadcasted_iota(jnp.int32, (LANES, LANES), 1)
    ahead = jnp.where(big0 < big1, 1.0, 0.0).astype(jnp.bfloat16)
    within = nn_dot(named16, ahead)
    counts = nn_dot(named16, jnp.ones((LANES, LANES), jnp.bfloat16)).astype(jnp.bfloat16)
    row_home = recode(lax.broadcasted_iota(jnp.int32, (MEMBERS, MEMBERS), 0) ^ my_code)
    col_home = recode(lax.broadcasted_iota(jnp.int32, (MEMBERS, MEMBERS), 1) ^ my_code)
    earlier = jnp.where(col_home < row_home, 1.0, 0.0).astype(jnp.bfloat16)
    position = within + nn_dot(earlier, counts)
    load = nn_dot(jnp.ones((MEMBERS, MEMBERS), jnp.bfloat16), counts)
    cap = capacity[0, 0].astype(jnp.float32)
    taken = jnp.minimum(cap - jnp.minimum(load, cap), float(OVF))
    dsend[0] = taken[0:1, :]
    for copy in spare_to:
        copy.start()

    for q in range(PARTS):
        gather(1, q, 2).wait_recv()
        gather(1, q, 3).start()

    limit = jnp.zeros((1, LANES), jnp.float32) + cap
    for b in range(levels):
        spare_to[b].wait_recv()
        limit += drecv[b] * (pair_mask[0] == 1 << b).astype(jnp.float32)
    gkeep[...] = jnp.where(position < limit, mat, 0.0)
    for j in range(MEMBERS):
        row = jnp.broadcast_to(gkeep[j : j + 1, :], (TOK, LANES))
        column = jnp.sum(jnp.where(lane == sub, row, 0.0), axis=1, keepdims=True)
        gcol[j * TOK : (j + 1) * TOK, :] = jnp.broadcast_to(column, (TOK, LANES))

    for q in range(PARTS):
        gather(0, q, 3).wait_recv()
    for copy in weights[:4]:
        copy.wait()

    def block(a, q):
        pieces = []
        for j in range(MEMBERS):
            p = PLACE[q][j]
            pieces.append(xb[a * PARTS + q, p * TOK : (p + 1) * TOK, :])
        return jnp.concatenate(pieces, axis=0)

    def forward_tile(n, carry):
        at = pl.multiple_of(n * TILE, TILE)
        up_at = pl.multiple_of(hidden + n * TILE, TILE)
        gate_pre = jnp.zeros((ROWS, TILE), jnp.float32)
        up_pre = jnp.zeros((ROWS, TILE), jnp.float32)
        for q in range(PARTS):
            lhs = block(0, q)
            rows = slice(q * part, (q + 1) * part)
            gate_pre += nn_dot(lhs, gu_v[rows, pl.ds(at, TILE)])
            up_pre += nn_dot(lhs, gu_v[rows, pl.ds(up_at, TILE)])
        ta[...] = gate_pre
        tb[...] = up_pre

        def rows_of(i, inner):
            rows = pl.ds(pl.multiple_of(i * CHUNK, CHUNK), CHUNK)
            a = ta[rows, :]
            b = tb[rows, :]
            sigma = jax.nn.sigmoid(a)
            swish = a * sigma
            both = swish * b
            cols = pl.ds(at, TILE)
            p1[rows, cols] = both
            p2[rows, cols] = swish
            p3[rows, cols] = b * sigma * (1.0 + a * (1.0 - sigma))
            g = gcol[rows, :]
            hid[rows, cols] = (both * jnp.concatenate([g, g], axis=1)).astype(jnp.bfloat16)
            return inner

        return lax.fori_loop(0, ROWS // CHUNK, rows_of, carry)

    lax.fori_loop(0, hidden // TILE, forward_tile, 0)

    def reduce(a, q, r):
        n = a * PARTS + q
        rows = slice(STEP_AT[r], STEP_AT[r] + STEP_ROWS[r])
        return pltpu.make_async_remote_copy(
            src_ref=sb.at[n, rows, :],
            dst_ref=rb.at[n, rows, :],
            send_sem=rs_send.at[n * 4 + r],
            recv_sem=rs_recv.at[n * 4 + r],
            device_id=member(1 << ORDER[q][3 - r]),
            device_id_type=MESH,
        )

    def permuted(ref, q):
        return jnp.concatenate(
            [ref[SLOT[q][p] * TOK : (SLOT[q][p] + 1) * TOK, :] for p in range(MEMBERS)], axis=0
        )

    def produce(a, q, ref, weight):
        n = a * PARTS + q
        tile = min(TILE, part)
        for c in range(part // tile):
            cols = slice(c * tile, (c + 1) * tile)
            rows = slice(q * part + c * tile, q * part + (c + 1) * tile)
            value = nt_dot(permuted(ref, q), weight[rows, :])
            sb[n, 0:HALF, cols] = value[HALF:, :].astype(jnp.bfloat16)
            acc[n, :, cols] = value[:HALF, :]
        reduce(a, q, 0).start()

    def pass_on(a, q, r):
        n = a * PARTS + q
        reduce(a, q, r - 1).wait_recv()
        size = STEP_ROWS[r]
        total = acc[n, size : 2 * size, :]
        for i in range(r):
            at = STEP_AT[i] + size
            total += rb[n, at : at + size, :].astype(jnp.float32)
        sb[n, STEP_AT[r] : STEP_AT[r] + size, :] = total.astype(jnp.bfloat16)
        reduce(a, q, r).start()

    def finish(a, q, ref):
        n = a * PARTS + q
        reduce(a, q, 3).wait_recv()
        total = acc[n, 0:TOK, :]
        for i in range(4):
            total += rb[n, STEP_AT[i] : STEP_AT[i] + TOK, :].astype(jnp.float32)
        ref[:, q * part : (q + 1) * part] = total.astype(jnp.bfloat16)

    for copy in weights[4:]:
        copy.wait()
    for q in range(PARTS):
        produce(0, q, hid, dn_v)

    for q in range(PARTS):
        gather(1, q, 3).wait_recv()
    ggacc[...] = jnp.zeros_like(ggacc)

    def backward_tile(n, carry):
        at = pl.multiple_of(n * TILE, TILE)
        up_at = pl.multiple_of(hidden + n * TILE, TILE)
        total = jnp.zeros((ROWS, TILE), jnp.float32)
        for q in range(PARTS):
            total += nn_dot(block(1, q), dn_v[q * part : (q + 1) * part, pl.ds(at, TILE)])
        ta[...] = total

        def rows_of(i, inner):
            rows = pl.ds(pl.multiple_of(i * CHUNK, CHUNK), CHUNK)
            cols = pl.ds(at, TILE)
            back = ta[rows, :]
            inner_terms = back * p1[rows, cols]
            ggacc[rows, :] += inner_terms[:, :LANES] + inner_terms[:, LANES:]
            g = gcol[rows, :]
            scaled = back * jnp.concatenate([g, g], axis=1)
            dpre[rows, cols] = (scaled * p3[rows, cols]).astype(jnp.bfloat16)
            dpre[rows, pl.ds(up_at, TILE)] = (scaled * p2[rows, cols]).astype(jnp.bfloat16)
            return inner

        return lax.fori_loop(0, ROWS // CHUNK, rows_of, carry)

    lax.fori_loop(0, hidden // TILE, backward_tile, 0)

    for q in range(PARTS):
        produce(1, q, dpre, gu_v)

    for j in range(MEMBERS):
        column = jnp.sum(ggacc[j * TOK : (j + 1) * TOK, :], axis=1, keepdims=True)
        row = jnp.sum(jnp.where(lane == sub, column, 0.0), axis=0, keepdims=True)
        qsend[j] = jnp.where(gkeep[j : j + 1, :] > 0.0, row, 0.0)
    for copy in quot_to:
        copy.start()

    for r in range(1, 4):
        for q in range(PARTS):
            pass_on(0, q, r)
        for q in range(PARTS):
            pass_on(1, q, r)

    gmat[0:1, :] = qsend[0]
    for j in range(1, MEMBERS):
        quot_to[j - 1].wait_recv()
        gmat[j : j + 1, :] = qrecv[j]
    square = jnp.concatenate(
        [gmat[...], jnp.zeros((LANES - MEMBERS, LANES), jnp.float32)], axis=0
    )
    by_token = square.T[:TOK, :]
    picked = jnp.zeros((TOK, LANES), jnp.float32)
    for k in range(TOPK):
        value = jnp.sum(
            jnp.where(lane == rel[:, k : k + 1], by_token, 0.0), axis=1, keepdims=True
        )
        picked += jnp.where(lane == k, value, 0.0)
    ggrad_ref[...] = picked[:, :TOPK]

    for q in range(PARTS):
        finish(0, q, out_ref)
    for q in range(PARTS):
        finish(1, q, igrad_ref)

    for a in range(2):
        for q in range(PARTS):
            for s in range(4):
                gather(a, q, s).wait_send()
                reduce(a, q, s).wait_send()
    for copy in gates_to + spare_to + quot_to:
        copy.wait_send()


def body(tokens, grad_out, gate_probs, routes, capacity, pair_mask, gate_up_weight, down_weight):
    width = tokens.shape[1]
    hidden = down_weight.shape[2]
    part = width // PARTS
    levels = lax.axis_size("dp").bit_length() - 1
    vmem = pl.BlockSpec(memory_space=pltpu.VMEM)
    smem = pl.BlockSpec(memory_space=pltpu.SMEM)
    anywhere = pl.BlockSpec(memory_space=pl.ANY)
    f32, b16 = jnp.float32, jnp.bfloat16
    dma = pltpu.SemaphoreType.DMA
    streams = 2 * PARTS
    return pl.pallas_call(
        functools.partial(kernel, levels),
        out_shape=(
            jax.ShapeDtypeStruct((TOK, width), b16),
            jax.ShapeDtypeStruct((TOK, width), b16),
            jax.ShapeDtypeStruct((TOK, TOPK), f32),
        ),
        in_specs=[anywhere, anywhere, vmem, vmem, smem, smem, anywhere, anywhere],
        out_specs=(vmem, vmem, vmem),
        scratch_shapes=[
            pltpu.VMEM((width, 2 * hidden), b16),
            pltpu.VMEM((width, hidden), b16),
            pltpu.VMEM((streams, ROWS, part), b16),
            pltpu.VMEM((streams, 240, part), b16),
            pltpu.VMEM((streams, 240, part), b16),
            pltpu.VMEM((streams, HALF, part), f32),
            pltpu.VMEM((ROWS, hidden), f32),
            pltpu.VMEM((ROWS, hidden), f32),
            pltpu.VMEM((ROWS, hidden), f32),
            pltpu.VMEM((ROWS, hidden), b16),
            pltpu.VMEM((ROWS, 2 * hidden), b16),
            pltpu.VMEM((ROWS, TILE), f32),
            pltpu.VMEM((ROWS, TILE), f32),
            pltpu.VMEM((MEMBERS, 1, LANES), f32),
            pltpu.VMEM((MEMBERS, 1, LANES), f32),
            pltpu.VMEM((MEMBERS, LANES), f32),
            pltpu.VMEM((MEMBERS, LANES), f32),
            pltpu.VMEM((ROWS, LANES), f32),
            pltpu.VMEM((ROWS, LANES), f32),
            pltpu.VMEM((MEMBERS, 1, LANES), f32),
            pltpu.VMEM((MEMBERS, 1, LANES), f32),
            pltpu.VMEM((1, 1, LANES), f32),
            pltpu.VMEM((max(levels, 1), 1, LANES), f32),
            dma((streams,)),
            dma((8,)),
            dma((streams * 4,)),
            dma((streams * 4,)),
            dma((streams * 4,)),
            dma((streams * 4,)),
            dma((MEMBERS,)),
            dma((MEMBERS,)),
            dma((MEMBERS,)),
            dma((MEMBERS,)),
            dma((max(levels, 1),)),
            dma((max(levels, 1),)),
        ],
        compiler_params=pltpu.CompilerParams(
            collective_id=0, has_side_effects=True, vmem_limit_bytes=48 * 1024 * 1024
        ),
        cost_estimate=pl.CostEstimate(
            flops=2 * ROWS * width * hidden * 6,
            bytes_accessed=width * hidden * 6,
            transcendentals=ROWS * hidden,
        ),
    )(tokens, grad_out, gate_probs, routes, capacity, pair_mask, gate_up_weight, down_weight)


def solution(mesh):
    rows = P(("dp", "expert"), None)
    return jax.shard_map(
        body,
        mesh=mesh,
        in_specs=(
            rows,
            rows,
            rows,
            rows,
            P("dp", "expert"),
            P("expert"),
            P("expert", None, None),
            P("expert", None, None),
        ),
        out_specs=(rows, rows, rows),
        check_vma=False,
    )
```

```python
import functools

import jax
import jax.numpy as jnp
from jax import lax
from jax.experimental import pallas as pl
from jax.experimental.pallas import tpu as pltpu
from jax.sharding import PartitionSpec as P

TOPK = 8
OVF = 16
MEMBERS = 16
TOK = 16
PARTS = 4
ROWS = MEMBERS * TOK
HALF = ROWS // 2
TILE = 256
CHUNK = 32
LANES = 128
RING_BIT = 3
MESH = pl.DeviceIdType.MESH

ORDER = [[(q + s) % 4 for s in range(4)] for q in range(PARTS)]


def slot_of(q, p):
    return sum(1 << ORDER[q][s] for s in range(4) if p >> s & 1)


PLACE = [{slot_of(q, p): p for p in range(MEMBERS)} for q in range(PARTS)]
SLOT = [[slot_of(q, p) for p in range(MEMBERS)] for q in range(PARTS)]
STEP_AT = [0, 128, 192, 224]
STEP_ROWS = [128, 64, 32, 16]


def flip(v, bits):
    if bits & 2:
        v = 3 - v
    if bits & 1:
        v = v + 1 - 2 * lax.rem(v, 2)
    return v


def recode(v):
    return v ^ ((v >> 1) & 5)


def nt_dot(a, b):
    return lax.dot_general(a, b, (((1,), (1,)), ((), ())), preferred_element_type=jnp.float32)


def nn_dot(a, b):
    return jnp.dot(a, b, preferred_element_type=jnp.float32)


def kernel(
    levels,
    tokens,
    grads,
    gates,
    routes,
    capacity,
    pair_mask,
    gate_up,
    down,
    out_ref,
    igrad_ref,
    ggrad_ref,
    gu_v,
    dn_v,
    xb,
    sb,
    rb,
    acc,
    p2,
    p3,
    hid,
    dpre,
    ta,
    tb,
    gates_v,
    routes_v,
    cap_s,
    mask_s,
    gsend,
    grecv,
    gmat,
    gkeep,
    gcol,
    ggacc,
    qsend,
    qrecv,
    dsend,
    drecv,
    local_sem,
    tiny_sem,
    weight_sem,
    ag_send,
    ag_recv,
    rs_send,
    rs_recv,
    g_send,
    g_recv,
    q_send,
    q_recv,
    d_send,
    d_recv,
):
    width = tokens.shape[1]
    part = width // PARTS
    hidden = down.shape[2]
    replicas = 1 << levels
    dp = lax.axis_index("dp")
    me = lax.axis_index("expert")
    mx, my = lax.div(me, 4), lax.rem(me, 4)

    def member(j):
        return (dp, flip(mx, j >> 2) * 4 + flip(my, j & 3))

    def moved(step):
        return (lax.rem(dp + step + replicas, replicas), me)

    def partner(b):
        step = 1 << b
        return (dp + step * (1 - 2 * lax.rem(lax.div(dp, step), 2)), me)

    direct = min(levels, RING_BIT)
    jump = 1 << RING_BIT
    far = (replicas // jump) // 2
    back_far = far // 2
    ways = [1] * (far > 0) + [-1] * (back_far > 0)

    tiny = [
        pltpu.make_async_copy(routes, routes_v, tiny_sem.at[0]),
        pltpu.make_async_copy(gates, gates_v, tiny_sem.at[1]),
        pltpu.make_async_copy(capacity, cap_s, tiny_sem.at[2]),
        pltpu.make_async_copy(pair_mask, mask_s, tiny_sem.at[3]),
    ]
    for copy in tiny:
        copy.start()
    barrier = pltpu.get_barrier_semaphore()
    everyone = [member(j) for j in range(1, MEMBERS)] + [partner(b) for b in range(direct)]
    if far > 1:
        everyone += [moved(jump), moved(-jump)]
    elif far:
        everyone += [moved(jump)]
    for other in everyone:
        pl.semaphore_signal(barrier, inc=1, device_id=other, device_id_type=MESH)

    sources = (tokens, grads)
    local = []
    for a in range(2):
        for q in range(PARTS):
            copy = pltpu.make_async_copy(
                sources[a].at[:, q * part : (q + 1) * part],
                xb.at[a * PARTS + q, 0:TOK, :],
                local_sem.at[a * PARTS + q],
            )
            copy.start()
            local.append(copy)
    weights = []
    for i in range(PARTS):
        rows = slice(i * part, (i + 1) * part)
        weights.append(
            pltpu.make_async_copy(gate_up.at[0, rows, :], gu_v.at[rows, :], weight_sem.at[i])
        )
    for i in range(PARTS):
        rows = slice(i * part, (i + 1) * part)
        weights.append(
            pltpu.make_async_copy(down.at[0, rows, :], dn_v.at[rows, :], weight_sem.at[4 + i])
        )
    for copy in weights:
        copy.start()

    my_code = recode(me)
    lane = lax.broadcasted_iota(jnp.int32, (TOK, LANES), 1)
    sub = lax.broadcasted_iota(jnp.int32, (TOK, LANES), 0)
    slots = lax.broadcasted_iota(jnp.int32, (MEMBERS, TOK), 0)
    for copy in tiny:
        copy.wait()
    rel = recode(routes_v[...]) ^ my_code
    gate_values = gates_v[...].astype(jnp.float32)
    dense = jnp.zeros((MEMBERS, TOK), jnp.float32)
    for k in range(TOPK):
        dense += jnp.where(slots == rel[k : k + 1, :], gate_values[k : k + 1, :], 0.0)
    gmat[...] = jnp.zeros_like(gmat)
    gmat[:, 0:TOK] = dense
    for j in range(MEMBERS):
        gsend[j] = gmat[j : j + 1, :]

    pl.semaphore_wait(barrier, len(everyone))

    def gather(a, q, s):
        n = a * PARTS + q
        held = TOK << s
        if s == 0:
            src = sources[a].at[:, q * part : (q + 1) * part]
        else:
            src = xb.at[n, 0:held, :]
        return pltpu.make_async_remote_copy(
            src_ref=src,
            dst_ref=xb.at[n, held : 2 * held, :],
            send_sem=ag_send.at[n * 4 + s],
            recv_sem=ag_recv.at[n * 4 + s],
            device_id=member(1 << ORDER[q][s]),
            device_id_type=MESH,
        )

    def small(src, dst, send, recv, index, slot, other):
        return pltpu.make_async_remote_copy(
            src_ref=src.at[index],
            dst_ref=dst.at[slot],
            send_sem=send.at[slot],
            recv_sem=recv.at[slot],
            device_id=other,
            device_id_type=MESH,
        )

    gates_to = [small(gsend, grecv, g_send, g_recv, j, j, member(j)) for j in range(1, MEMBERS)]
    direct_to = [small(dsend, drecv, d_send, d_recv, 0, b, partner(b)) for b in range(direct)]

    def ring_slot(way, d):
        return direct + d - 1 + (far if way < 0 else 0)

    def ring_hop(way, d):
        src, index = (dsend, 0) if d == 1 else (drecv, ring_slot(way, d - 1))
        return small(src, drecv, d_send, d_recv, index, ring_slot(way, d), moved(way * jump))

    hops = {(1, d): ring_hop(1, d) for d in range(1, far + 1)}
    hops.update({(-1, d): ring_hop(-1, d) for d in range(1, back_far + 1)})

    def ring_round(d):
        for way in ways:
            if (way, d) in hops:
                if d > 1:
                    hops[way, d - 1].wait_recv()
                hops[way, d].start()

    quot_to = [small(qsend, qrecv, q_send, q_recv, j, j, member(j)) for j in range(1, MEMBERS)]

    def step_on(a, s):
        for q in range(PARTS):
            gather(a, q, s - 1).wait_recv()
            gather(a, q, s).start()

    for q in range(PARTS):
        gather(0, q, 0).start()
    for copy in gates_to:
        copy.start()
    for q in range(PARTS):
        gather(1, q, 0).start()
    for copy in local:
        copy.wait()
    step_on(0, 1)
    step_on(1, 1)

    gmat[0:1, :] = gsend[0]
    for j in range(1, MEMBERS):
        gates_to[j - 1].wait_recv()
        gmat[j : j + 1, :] = grecv[j]
    mat = gmat[...]
    named16 = jnp.where(mat > 0.0, 1.0, 0.0).astype(jnp.bfloat16)
    counts = nn_dot(named16, jnp.ones((LANES, LANES), jnp.bfloat16)).astype(jnp.bfloat16)
    load = nn_dot(jnp.ones((MEMBERS, MEMBERS), jnp.bfloat16), counts)
    cap = jnp.broadcast_to(cap_s[...].astype(jnp.float32), (1, LANES))
    taken = jnp.minimum(cap - jnp.minimum(load, cap), float(OVF))
    dsend[0] = taken[0:1, :]
    ring_round(1)
    for copy in direct_to:
        copy.start()

    step_on(0, 2)
    step_on(1, 2)
    big0 = lax.broadcasted_iota(jnp.int32, (LANES, LANES), 0)
    big1 = lax.broadcasted_iota(jnp.int32, (LANES, LANES), 1)
    ahead = jnp.where(big0 < big1, 1.0, 0.0).astype(jnp.bfloat16)
    within = nn_dot(named16, ahead)
    row_home = recode(lax.broadcasted_iota(jnp.int32, (MEMBERS, MEMBERS), 0) ^ my_code)
    col_home = recode(lax.broadcasted_iota(jnp.int32, (MEMBERS, MEMBERS), 1) ^ my_code)
    earlier = jnp.where(col_home < row_home, 1.0, 0.0).astype(jnp.bfloat16)
    position = within + nn_dot(earlier, counts)
    ring_round(2)
    step_on(0, 3)
    ring_round(3)
    step_on(1, 3)
    ring_round(4)

    for q in range(PARTS):
        gather(0, q, 3).wait_recv()
    for copy in weights[:4]:
        copy.wait()

    def block(a, q):
        pieces = []
        for j in range(MEMBERS):
            p = PLACE[q][j]
            pieces.append(xb[a * PARTS + q, p * TOK : (p + 1) * TOK, :])
        return jnp.concatenate(pieces, axis=0)

    def forward_tile(n, carry):
        at = pl.multiple_of(n * TILE, TILE)
        up_at = pl.multiple_of(hidden + n * TILE, TILE)
        gate_pre = jnp.zeros((ROWS, TILE), jnp.float32)
        up_pre = jnp.zeros((ROWS, TILE), jnp.float32)
        for q in range(PARTS):
            lhs = block(0, q)
            rows = slice(q * part, (q + 1) * part)
            gate_pre += nn_dot(lhs, gu_v[rows, pl.ds(at, TILE)])
            up_pre += nn_dot(lhs, gu_v[rows, pl.ds(up_at, TILE)])
        ta[...] = gate_pre
        tb[...] = up_pre

        def rows_of(i, inner):
            rows = pl.ds(pl.multiple_of(i * CHUNK, CHUNK), CHUNK)
            a = ta[rows, :]
            b = tb[rows, :]
            sigma = jax.nn.sigmoid(a)
            swish = a * sigma
            both = swish * b
            cols = pl.ds(at, TILE)
            p2[rows, cols] = swish
            p3[rows, cols] = b * sigma * (1.0 + a * (1.0 - sigma))
            hid[rows, cols] = both.astype(jnp.bfloat16)
            return inner

        return lax.fori_loop(0, ROWS // CHUNK, rows_of, carry)

    lax.fori_loop(0, hidden // TILE, forward_tile, 0)

    limit = jnp.zeros((1, LANES), jnp.float32) + cap
    for b in range(direct):
        direct_to[b].wait_recv()
        limit += drecv[b] * (mask_s[...] == 1 << b).astype(jnp.float32)
    for way, d in hops:
        if (way, d + 1) not in hops:
            hops[way, d].wait_recv()
    for b in range(direct, levels):
        d = 1 << (b - direct)
        wanted = (mask_s[...] == 1 << b).astype(jnp.float32)
        behind = drecv[ring_slot(1, d)]
        if d < far:
            upper = lax.rem(lax.div(dp, 1 << b), 2).astype(jnp.float32)
            behind = upper * behind + (1.0 - upper) * drecv[ring_slot(-1, d)]
        limit += wanted * behind
    gkeep[...] = jnp.where(position < limit, mat, 0.0)
    for j in range(MEMBERS):
        row = jnp.broadcast_to(gkeep[j : j + 1, :], (TOK, LANES))
        column = jnp.sum(jnp.where(lane == sub, row, 0.0), axis=1, keepdims=True)
        gcol[j * TOK : (j + 1) * TOK, :] = jnp.broadcast_to(column, (TOK, LANES))

    def reduce(a, q, r):
        n = a * PARTS + q
        rows = slice(STEP_AT[r], STEP_AT[r] + STEP_ROWS[r])
        return pltpu.make_async_remote_copy(
            src_ref=sb.at[n, rows, :],
            dst_ref=rb.at[n, rows, :],
            send_sem=rs_send.at[n * 4 + r],
            recv_sem=rs_recv.at[n * 4 + r],
            device_id=member(1 << ORDER[q][3 - r]),
            device_id_type=MESH,
        )

    def permuted(ref, q):
        return jnp.concatenate(
            [ref[SLOT[q][p] * TOK : (SLOT[q][p] + 1) * TOK, :] for p in range(MEMBERS)], axis=0
        )

    def produce(a, q, ref, weight):
        n = a * PARTS + q
        tile = min(TILE, part)
        gate = permuted(gcol, q)
        gate = jnp.concatenate([gate] * (tile // LANES), axis=1)
        for c in range(part // tile):
            cols = slice(c * tile, (c + 1) * tile)
            rows = slice(q * part + c * tile, q * part + (c + 1) * tile)
            value = nt_dot(permuted(ref, q), weight[rows, :]) * gate
            sb[n, 0:HALF, cols] = value[HALF:, :].astype(jnp.bfloat16)
            acc[n, :, cols] = value[:HALF, :]
        reduce(a, q, 0).start()

    def pass_on(a, q, r):
        n = a * PARTS + q
        reduce(a, q, r - 1).wait_recv()
        size = STEP_ROWS[r]
        total = acc[n, size : 2 * size, :]
        for i in range(r):
            at = STEP_AT[i] + size
            total += rb[n, at : at + size, :].astype(jnp.float32)
        sb[n, STEP_AT[r] : STEP_AT[r] + size, :] = total.astype(jnp.bfloat16)
        reduce(a, q, r).start()

    def finish(a, q, ref):
        n = a * PARTS + q
        reduce(a, q, 3).wait_recv()
        total = acc[n, 0:TOK, :]
        for i in range(4):
            total += rb[n, STEP_AT[i] : STEP_AT[i] + TOK, :].astype(jnp.float32)
        ref[:, q * part : (q + 1) * part] = total.astype(jnp.bfloat16)

    for copy in weights[4:]:
        copy.wait()
    for q in range(PARTS):
        produce(0, q, hid, dn_v)

    for q in range(PARTS):
        gather(1, q, 3).wait_recv()
    ggacc[...] = jnp.zeros_like(ggacc)

    def backward_tile(n, carry):
        at = pl.multiple_of(n * TILE, TILE)
        up_at = pl.multiple_of(hidden + n * TILE, TILE)
        total = jnp.zeros((ROWS, TILE), jnp.float32)
        for q in range(PARTS):
            total += nn_dot(block(1, q), dn_v[q * part : (q + 1) * part, pl.ds(at, TILE)])
        ta[...] = total

        def rows_of(i, inner):
            rows = pl.ds(pl.multiple_of(i * CHUNK, CHUNK), CHUNK)
            cols = pl.ds(at, TILE)
            back = ta[rows, :]
            terms = back * hid[rows, cols].astype(jnp.float32)
            ggacc[rows, :] += terms[:, :LANES] + terms[:, LANES:]
            dpre[rows, cols] = (back * p3[rows, cols]).astype(jnp.bfloat16)
            dpre[rows, pl.ds(up_at, TILE)] = (back * p2[rows, cols]).astype(jnp.bfloat16)
            return inner

        return lax.fori_loop(0, ROWS // CHUNK, rows_of, carry)

    lax.fori_loop(0, hidden // TILE, backward_tile, 0)

    for q in range(PARTS):
        produce(1, q, dpre, gu_v)

    for j in range(MEMBERS):
        column = jnp.sum(ggacc[j * TOK : (j + 1) * TOK, :], axis=1, keepdims=True)
        row = jnp.sum(jnp.where(lane == sub, column, 0.0), axis=0, keepdims=True)
        qsend[j] = jnp.where(gkeep[j : j + 1, :] > 0.0, row, 0.0)
    for copy in quot_to:
        copy.start()

    for r in range(1, 4):
        for q in range(PARTS):
            pass_on(0, q, r)
        for q in range(PARTS):
            pass_on(1, q, r)

    gmat[0:1, :] = qsend[0]
    for j in range(1, MEMBERS):
        quot_to[j - 1].wait_recv()
        gmat[j : j + 1, :] = qrecv[j]
    by_slot = gmat[:, 0:TOK]
    for k in range(TOPK):
        ggrad_ref[k : k + 1, :] = jnp.sum(
            jnp.where(slots == rel[k : k + 1, :], by_slot, 0.0), axis=0, keepdims=True
        )

    for q in range(PARTS):
        finish(0, q, out_ref)
    for q in range(PARTS):
        finish(1, q, igrad_ref)

    for a in range(2):
        for q in range(PARTS):
            for s in range(4):
                gather(a, q, s).wait_send()
                reduce(a, q, s).wait_send()
    for copy in gates_to + direct_to + list(hops.values()) + quot_to:
        copy.wait_send()


def body(tokens, grad_out, gate_probs, routes, capacity, pair_mask, gate_up_weight, down_weight):
    width = tokens.shape[1]
    hidden = down_weight.shape[2]
    part = width // PARTS
    levels = lax.axis_size("dp").bit_length() - 1
    vmem = pl.BlockSpec(memory_space=pltpu.VMEM)
    in_hbm = pl.BlockSpec(memory_space=pltpu.HBM)
    f32, b16 = jnp.float32, jnp.bfloat16
    dma = pltpu.SemaphoreType.DMA
    streams = 2 * PARTS
    out, igrad, ggrad = pl.pallas_call(
        functools.partial(kernel, levels),
        out_shape=(
            jax.ShapeDtypeStruct((TOK, width), b16),
            jax.ShapeDtypeStruct((TOK, width), b16),
            jax.ShapeDtypeStruct((TOPK, TOK), f32),
        ),
        in_specs=[in_hbm] * 8,
        out_specs=(vmem, vmem, vmem),
        scratch_shapes=[
            pltpu.VMEM((width, 2 * hidden), b16),
            pltpu.VMEM((width, hidden), b16),
            pltpu.VMEM((streams, ROWS, part), b16),
            pltpu.VMEM((streams, 240, part), b16),
            pltpu.VMEM((streams, 240, part), b16),
            pltpu.VMEM((streams, HALF, part), f32),
            pltpu.VMEM((ROWS, hidden), f32),
            pltpu.VMEM((ROWS, hidden), f32),
            pltpu.VMEM((ROWS, hidden), b16),
            pltpu.VMEM((ROWS, 2 * hidden), b16),
            pltpu.VMEM((ROWS, TILE), f32),
            pltpu.VMEM((ROWS, TILE), f32),
            pltpu.VMEM((TOPK, TOK), b16),
            pltpu.VMEM((TOPK, TOK), jnp.int32),
            pltpu.VMEM((1, 1), jnp.int32),
            pltpu.VMEM((1, 1), jnp.int32),
            pltpu.VMEM((MEMBERS, 1, LANES), f32),
            pltpu.VMEM((MEMBERS, 1, LANES), f32),
            pltpu.VMEM((MEMBERS, LANES), f32),
            pltpu.VMEM((MEMBERS, LANES), f32),
            pltpu.VMEM((ROWS, LANES), f32),
            pltpu.VMEM((ROWS, LANES), f32),
            pltpu.VMEM((MEMBERS, 1, LANES), f32),
            pltpu.VMEM((MEMBERS, 1, LANES), f32),
            pltpu.VMEM((1, 1, LANES), f32),
            pltpu.VMEM((16, 1, LANES), f32),
            dma((streams,)),
            dma((4,)),
            dma((8,)),
            dma((streams * 4,)),
            dma((streams * 4,)),
            dma((streams * 4,)),
            dma((streams * 4,)),
            dma((MEMBERS,)),
            dma((MEMBERS,)),
            dma((MEMBERS,)),
            dma((MEMBERS,)),
            dma((16,)),
            dma((16,)),
        ],
        compiler_params=pltpu.CompilerParams(
            collective_id=0, has_side_effects=True, vmem_limit_bytes=60 * 1024 * 1024
        ),
        cost_estimate=pl.CostEstimate(
            flops=2 * ROWS * width * hidden * 6,
            bytes_accessed=width * hidden * 6,
            transcendentals=ROWS * hidden,
        ),
    )(
        tokens,
        grad_out,
        gate_probs.T,
        routes.T,
        capacity,
        pair_mask.reshape(1, 1),
        gate_up_weight,
        down_weight,
    )
    return (out, igrad, ggrad.T)


def solution(mesh):
    rows = P(("dp", "expert"), None)
    return jax.shard_map(
        body,
        mesh=mesh,
        in_specs=(
            rows,
            rows,
            rows,
            rows,
            P("dp", "expert"),
            P("expert"),
            P("expert", None, None),
            P("expert", None, None),
        ),
        out_specs=(rows, rows, rows),
        check_vma=False,
    )
```

```python
import functools

import jax
import jax.numpy as jnp
from jax import lax
from jax.experimental import pallas as pl
from jax.experimental.pallas import tpu as pltpu
from jax.sharding import PartitionSpec as P

TOPK = 8
OVF = 16
MEMBERS = 16
TOK = 16
PARTS = 4
ROWS = MEMBERS * TOK
HALF = ROWS // 2
TILE = 256
CHUNK = 32
LANES = 128
MESH = pl.DeviceIdType.MESH

ORDER = [[(q + s) % 4 for s in range(4)] for q in range(PARTS)]


def slot_of(q, p):
    return sum(1 << ORDER[q][s] for s in range(4) if p >> s & 1)


PLACE = [{slot_of(q, p): p for p in range(MEMBERS)} for q in range(PARTS)]
SLOT = [[slot_of(q, p) for p in range(MEMBERS)] for q in range(PARTS)]
STEP_AT = [0, 128, 192, 224]
STEP_ROWS = [128, 64, 32, 16]


def flip(v, bits):
    if bits & 2:
        v = 3 - v
    if bits & 1:
        v = v + 1 - 2 * lax.rem(v, 2)
    return v


def recode(v):
    return v ^ ((v >> 1) & 5)


def nt_dot(a, b):
    return lax.dot_general(a, b, (((1,), (1,)), ((), ())), preferred_element_type=jnp.float32)


def nn_dot(a, b):
    return jnp.dot(a, b, preferred_element_type=jnp.float32)


def kernel(
    levels,
    tokens,
    grads,
    gates,
    routes,
    capacity,
    pair_mask,
    gate_up,
    down,
    out_ref,
    igrad_ref,
    ggrad_ref,
    gu_v,
    dn_v,
    xb,
    sb,
    rb,
    acc,
    p2,
    p3,
    hid,
    dpre,
    ta,
    tb,
    gates_v,
    routes_v,
    cap_s,
    mask_s,
    gsend,
    grecv,
    gmat,
    gkeep,
    gcol,
    ggacc,
    qsend,
    qrecv,
    dsend,
    drecv,
    local_sem,
    tiny_sem,
    weight_sem,
    ag_send,
    ag_recv,
    rs_send,
    rs_recv,
    g_send,
    g_recv,
    q_send,
    q_recv,
    d_send,
    d_recv,
):
    width = tokens.shape[1]
    part = width // PARTS
    hidden = down.shape[2]
    dp = lax.axis_index("dp")
    me = lax.axis_index("expert")
    mx, my = lax.div(me, 4), lax.rem(me, 4)

    def member(j):
        return (dp, flip(mx, j >> 2) * 4 + flip(my, j & 3))

    def bit(b):
        return lax.rem(lax.div(dp, 1 << b), 2)

    def partner(b):
        return (dp + (1 << b) * (1 - 2 * bit(b)), me)

    tiny = [
        pltpu.make_async_copy(routes, routes_v, tiny_sem.at[0]),
        pltpu.make_async_copy(gates, gates_v, tiny_sem.at[1]),
        pltpu.make_async_copy(capacity, cap_s, tiny_sem.at[2]),
        pltpu.make_async_copy(pair_mask, mask_s, tiny_sem.at[3]),
    ]
    for copy in tiny:
        copy.start()
    barrier = pltpu.get_barrier_semaphore()
    for j in range(1, MEMBERS):
        pl.semaphore_signal(barrier, inc=1, device_id=member(j), device_id_type=MESH)
    heard = MEMBERS - 1
    for b in range(levels):
        heard = heard + bit(b)

        @pl.when(bit(b) == 0)
        def _():
            pl.semaphore_signal(barrier, inc=1, device_id=partner(b), device_id_type=MESH)

    sources = (tokens, grads)
    local = []
    for a in range(2):
        for q in range(PARTS):
            copy = pltpu.make_async_copy(
                sources[a].at[:, q * part : (q + 1) * part],
                xb.at[a * PARTS + q, 0:TOK, :],
                local_sem.at[a * PARTS + q],
            )
            copy.start()
            local.append(copy)
    weights = []
    for i in range(PARTS):
        rows = slice(i * part, (i + 1) * part)
        weights.append(
            pltpu.make_async_copy(gate_up.at[0, rows, :], gu_v.at[rows, :], weight_sem.at[i])
        )
    for i in range(PARTS):
        rows = slice(i * part, (i + 1) * part)
        weights.append(
            pltpu.make_async_copy(down.at[0, rows, :], dn_v.at[rows, :], weight_sem.at[4 + i])
        )
    for copy in weights:
        copy.start()

    my_code = recode(me)
    lane = lax.broadcasted_iota(jnp.int32, (TOK, LANES), 1)
    sub = lax.broadcasted_iota(jnp.int32, (TOK, LANES), 0)
    slots = lax.broadcasted_iota(jnp.int32, (MEMBERS, TOK), 0)
    for copy in tiny:
        copy.wait()
    rel = recode(routes_v[...]) ^ my_code
    gate_values = gates_v[...].astype(jnp.float32)
    dense = jnp.zeros((MEMBERS, TOK), jnp.float32)
    for k in range(TOPK):
        dense += jnp.where(slots == rel[k : k + 1, :], gate_values[k : k + 1, :], 0.0)
    gmat[...] = jnp.zeros_like(gmat)
    gmat[:, 0:TOK] = dense
    for j in range(MEMBERS):
        gsend[j] = gmat[j : j + 1, :]

    pl.semaphore_wait(barrier, heard)

    def gather(a, q, s):
        n = a * PARTS + q
        held = TOK << s
        if s == 0:
            src = sources[a].at[:, q * part : (q + 1) * part]
        else:
            src = xb.at[n, 0:held, :]
        return pltpu.make_async_remote_copy(
            src_ref=src,
            dst_ref=xb.at[n, held : 2 * held, :],
            send_sem=ag_send.at[n * 4 + s],
            recv_sem=ag_recv.at[n * 4 + s],
            device_id=member(1 << ORDER[q][s]),
            device_id_type=MESH,
        )

    def small(src, dst, send, recv, index, slot, other):
        return pltpu.make_async_remote_copy(
            src_ref=src.at[index],
            dst_ref=dst.at[slot],
            send_sem=send.at[slot],
            recv_sem=recv.at[slot],
            device_id=other,
            device_id_type=MESH,
        )

    gates_to = [small(gsend, grecv, g_send, g_recv, j, j, member(j)) for j in range(1, MEMBERS)]
    spare_to = [small(dsend, drecv, d_send, d_recv, 0, b, partner(b)) for b in range(levels)]
    quot_to = [small(qsend, qrecv, q_send, q_recv, j, j, member(j)) for j in range(1, MEMBERS)]

    def step_on(a, s):
        for q in range(PARTS):
            gather(a, q, s - 1).wait_recv()
            gather(a, q, s).start()

    for copy in gates_to:
        copy.start()
    for a in range(2):
        for q in range(PARTS):
            gather(a, q, 0).start()

    gmat[0:1, :] = gsend[0]
    for j in range(1, MEMBERS):
        gates_to[j - 1].wait_recv()
        gmat[j : j + 1, :] = grecv[j]
    mat = gmat[...]
    named16 = jnp.where(mat > 0.0, 1.0, 0.0).astype(jnp.bfloat16)
    counts = nn_dot(named16, jnp.ones((LANES, LANES), jnp.bfloat16)).astype(jnp.bfloat16)
    load = nn_dot(jnp.ones((MEMBERS, MEMBERS), jnp.bfloat16), counts)
    cap = jnp.broadcast_to(cap_s[...].astype(jnp.float32), (1, LANES))
    taken = jnp.minimum(cap - jnp.minimum(load, cap), float(OVF))
    dsend[0] = taken[0:1, :]
    for b in range(levels):

        @pl.when(bit(b) == 1)
        def _():
            spare_to[b].start()

    for copy in local:
        copy.wait()
    for s in range(1, 4):
        step_on(0, s)
        step_on(1, s)
    big0 = lax.broadcasted_iota(jnp.int32, (LANES, LANES), 0)
    big1 = lax.broadcasted_iota(jnp.int32, (LANES, LANES), 1)
    ahead = jnp.where(big0 < big1, 1.0, 0.0).astype(jnp.bfloat16)
    within = nn_dot(named16, ahead)
    row_home = recode(lax.broadcasted_iota(jnp.int32, (MEMBERS, MEMBERS), 0) ^ my_code)
    col_home = recode(lax.broadcasted_iota(jnp.int32, (MEMBERS, MEMBERS), 1) ^ my_code)
    earlier = jnp.where(col_home < row_home, 1.0, 0.0).astype(jnp.bfloat16)
    position = within + nn_dot(earlier, counts)
    for q in range(PARTS):
        gather(0, q, 3).wait_recv()
    for copy in weights[:4]:
        copy.wait()

    def block(a, q):
        pieces = []
        for j in range(MEMBERS):
            p = PLACE[q][j]
            pieces.append(xb[a * PARTS + q, p * TOK : (p + 1) * TOK, :])
        return jnp.concatenate(pieces, axis=0)

    def forward_tile(n, carry):
        at = pl.multiple_of(n * TILE, TILE)
        up_at = pl.multiple_of(hidden + n * TILE, TILE)
        gate_pre = jnp.zeros((ROWS, TILE), jnp.float32)
        up_pre = jnp.zeros((ROWS, TILE), jnp.float32)
        for q in range(PARTS):
            lhs = block(0, q)
            rows = slice(q * part, (q + 1) * part)
            gate_pre += nn_dot(lhs, gu_v[rows, pl.ds(at, TILE)])
            up_pre += nn_dot(lhs, gu_v[rows, pl.ds(up_at, TILE)])
        ta[...] = gate_pre
        tb[...] = up_pre

        def rows_of(i, inner):
            rows = pl.ds(pl.multiple_of(i * CHUNK, CHUNK), CHUNK)
            a = ta[rows, :]
            b = tb[rows, :]
            sigma = jax.nn.sigmoid(a)
            swish = a * sigma
            both = swish * b
            cols = pl.ds(at, TILE)
            p2[rows, cols] = swish
            p3[rows, cols] = b * sigma * (1.0 + a * (1.0 - sigma))
            hid[rows, cols] = both.astype(jnp.bfloat16)
            return inner

        return lax.fori_loop(0, ROWS // CHUNK, rows_of, carry)

    lax.fori_loop(0, hidden // TILE, forward_tile, 0)

    def reduce(a, q, r):
        n = a * PARTS + q
        rows = slice(STEP_AT[r], STEP_AT[r] + STEP_ROWS[r])
        return pltpu.make_async_remote_copy(
            src_ref=sb.at[n, rows, :],
            dst_ref=rb.at[n, rows, :],
            send_sem=rs_send.at[n * 4 + r],
            recv_sem=rs_recv.at[n * 4 + r],
            device_id=member(1 << ORDER[q][3 - r]),
            device_id_type=MESH,
        )

    def permuted(ref, q):
        return jnp.concatenate(
            [ref[SLOT[q][p] * TOK : (SLOT[q][p] + 1) * TOK, :] for p in range(MEMBERS)], axis=0
        )

    def produce(a, q, ref, weight):
        n = a * PARTS + q
        tile = min(TILE, part)
        for c in range(part // tile):
            cols = slice(c * tile, (c + 1) * tile)
            rows = slice(q * part + c * tile, q * part + (c + 1) * tile)
            acc[n, :, cols] = nt_dot(permuted(ref, q), weight[rows, :])

    def pass_on(a, q, r):
        n = a * PARTS + q
        reduce(a, q, r - 1).wait_recv()
        size = STEP_ROWS[r]
        total = acc[n, size : 2 * size, :] * gate_rows(q, size // TOK, size // TOK)
        for i in range(r):
            at = STEP_AT[i] + size
            total += rb[n, at : at + size, :].astype(jnp.float32)
        sb[n, STEP_AT[r] : STEP_AT[r] + size, :] = total.astype(jnp.bfloat16)
        reduce(a, q, r).start()

    def finish(a, q, ref):
        n = a * PARTS + q
        reduce(a, q, 3).wait_recv()
        total = acc[n, 0:TOK, :] * gate_rows(q, 0, 1)
        for i in range(4):
            total += rb[n, STEP_AT[i] : STEP_AT[i] + TOK, :].astype(jnp.float32)
        ref[:, q * part : (q + 1) * part] = total.astype(jnp.bfloat16)

    for copy in weights[4:]:
        copy.wait()
    for q in range(PARTS):
        produce(0, q, hid, dn_v)

    for q in range(PARTS):
        gather(1, q, 3).wait_recv()
    ggacc[...] = jnp.zeros_like(ggacc)

    def backward_tile(n, carry):
        at = pl.multiple_of(n * TILE, TILE)
        up_at = pl.multiple_of(hidden + n * TILE, TILE)
        total = jnp.zeros((ROWS, TILE), jnp.float32)
        for q in range(PARTS):
            total += nn_dot(block(1, q), dn_v[q * part : (q + 1) * part, pl.ds(at, TILE)])
        ta[...] = total

        def rows_of(i, inner):
            rows = pl.ds(pl.multiple_of(i * CHUNK, CHUNK), CHUNK)
            cols = pl.ds(at, TILE)
            back = ta[rows, :]
            terms = back * hid[rows, cols].astype(jnp.float32)
            ggacc[rows, :] += terms[:, :LANES] + terms[:, LANES:]
            dpre[rows, cols] = (back * p3[rows, cols]).astype(jnp.bfloat16)
            dpre[rows, pl.ds(up_at, TILE)] = (back * p2[rows, cols]).astype(jnp.bfloat16)
            return inner

        return lax.fori_loop(0, ROWS // CHUNK, rows_of, carry)

    lax.fori_loop(0, hidden // TILE, backward_tile, 0)

    for q in range(PARTS):
        produce(1, q, dpre, gu_v)

    for b in range(levels):

        @pl.when(bit(b) == 0)
        def _():
            spare_to[b].wait_recv()
            spare_to[b].start()

    for b in range(levels):

        @pl.when(bit(b) == 1)
        def _():
            spare_to[b].wait_recv()

    limit = cap
    for b in range(levels):
        limit += drecv[b] * (mask_s[...] == 1 << b).astype(jnp.float32)
    gkeep[...] = jnp.where(position < limit, mat, 0.0)
    for j in range(MEMBERS):
        row = jnp.broadcast_to(gkeep[j : j + 1, :], (TOK, LANES))
        column = jnp.sum(jnp.where(lane == sub, row, 0.0), axis=1, keepdims=True)
        gcol[j * TOK : (j + 1) * TOK, :] = jnp.broadcast_to(column, (TOK, LANES))

    def gate_rows(q, first, count):
        rows = [gcol[SLOT[q][p] * TOK : (SLOT[q][p] + 1) * TOK, :] for p in range(first, first + count)]
        return jnp.concatenate([jnp.concatenate(rows, axis=0)] * (part // LANES), axis=1)

    for a in range(2):
        for q in range(PARTS):
            n = a * PARTS + q
            for p in range(MEMBERS // 2, MEMBERS):
                rows = slice(p * TOK, (p + 1) * TOK)
                scaled = acc[n, rows, :] * gate_rows(q, p, 1)
                sb[n, p * TOK - HALF : (p + 1) * TOK - HALF, :] = scaled.astype(jnp.bfloat16)
            reduce(a, q, 0).start()

    for j in range(MEMBERS):
        column = jnp.sum(ggacc[j * TOK : (j + 1) * TOK, :], axis=1, keepdims=True)
        row = jnp.sum(jnp.where(lane == sub, column, 0.0), axis=0, keepdims=True)
        qsend[j] = jnp.where(gkeep[j : j + 1, :] > 0.0, row, 0.0)
    for copy in quot_to:
        copy.start()

    for r in range(1, 4):
        for q in range(PARTS):
            pass_on(0, q, r)
        for q in range(PARTS):
            pass_on(1, q, r)

    gmat[0:1, :] = qsend[0]
    for j in range(1, MEMBERS):
        quot_to[j - 1].wait_recv()
        gmat[j : j + 1, :] = qrecv[j]
    by_slot = gmat[:, 0:TOK]
    for k in range(TOPK):
        ggrad_ref[k : k + 1, :] = jnp.sum(
            jnp.where(slots == rel[k : k + 1, :], by_slot, 0.0), axis=0, keepdims=True
        )

    for q in range(PARTS):
        finish(0, q, out_ref)
    for q in range(PARTS):
        finish(1, q, igrad_ref)

    for a in range(2):
        for q in range(PARTS):
            for s in range(4):
                gather(a, q, s).wait_send()
                reduce(a, q, s).wait_send()
    for copy in gates_to + spare_to + quot_to:
        copy.wait_send()


def body(tokens, grad_out, gate_probs, routes, capacity, pair_mask, gate_up_weight, down_weight):
    width = tokens.shape[1]
    hidden = down_weight.shape[2]
    part = width // PARTS
    levels = lax.axis_size("dp").bit_length() - 1
    vmem = pl.BlockSpec(memory_space=pltpu.VMEM)
    in_hbm = pl.BlockSpec(memory_space=pltpu.HBM)
    f32, b16 = jnp.float32, jnp.bfloat16
    dma = pltpu.SemaphoreType.DMA
    streams = 2 * PARTS
    out, igrad, ggrad = pl.pallas_call(
        functools.partial(kernel, levels),
        out_shape=(
            jax.ShapeDtypeStruct((TOK, width), b16),
            jax.ShapeDtypeStruct((TOK, width), b16),
            jax.ShapeDtypeStruct((TOPK, TOK), f32),
        ),
        in_specs=[in_hbm] * 8,
        out_specs=(vmem, vmem, vmem),
        scratch_shapes=[
            pltpu.VMEM((width, 2 * hidden), b16),
            pltpu.VMEM((width, hidden), b16),
            pltpu.VMEM((streams, ROWS, part), b16),
            pltpu.VMEM((streams, 240, part), b16),
            pltpu.VMEM((streams, 240, part), b16),
            pltpu.VMEM((streams, ROWS, part), f32),
            pltpu.VMEM((ROWS, hidden), f32),
            pltpu.VMEM((ROWS, hidden), f32),
            pltpu.VMEM((ROWS, hidden), b16),
            pltpu.VMEM((ROWS, 2 * hidden), b16),
            pltpu.VMEM((ROWS, TILE), f32),
            pltpu.VMEM((ROWS, TILE), f32),
            pltpu.VMEM((TOPK, TOK), b16),
            pltpu.VMEM((TOPK, TOK), jnp.int32),
            pltpu.VMEM((1, 1), jnp.int32),
            pltpu.VMEM((1, 1), jnp.int32),
            pltpu.VMEM((MEMBERS, 1, LANES), f32),
            pltpu.VMEM((MEMBERS, 1, LANES), f32),
            pltpu.VMEM((MEMBERS, LANES), f32),
            pltpu.VMEM((MEMBERS, LANES), f32),
            pltpu.VMEM((ROWS, LANES), f32),
            pltpu.VMEM((ROWS, LANES), f32),
            pltpu.VMEM((MEMBERS, 1, LANES), f32),
            pltpu.VMEM((MEMBERS, 1, LANES), f32),
            pltpu.VMEM((1, 1, LANES), f32),
            pltpu.VMEM((16, 1, LANES), f32),
            dma((streams,)),
            dma((4,)),
            dma((8,)),
            dma((streams * 4,)),
            dma((streams * 4,)),
            dma((streams * 4,)),
            dma((streams * 4,)),
            dma((MEMBERS,)),
            dma((MEMBERS,)),
            dma((MEMBERS,)),
            dma((MEMBERS,)),
            dma((16,)),
            dma((16,)),
        ],
        compiler_params=pltpu.CompilerParams(
            collective_id=0, has_side_effects=True, vmem_limit_bytes=60 * 1024 * 1024
        ),
        cost_estimate=pl.CostEstimate(
            flops=2 * ROWS * width * hidden * 6,
            bytes_accessed=width * hidden * 6,
            transcendentals=ROWS * hidden,
        ),
    )(
        tokens,
        grad_out,
        gate_probs.T,
        routes.T,
        capacity,
        pair_mask.reshape(1, 1),
        gate_up_weight,
        down_weight,
    )
    return (out, igrad, ggrad.T)


def solution(mesh):
    rows = P(("dp", "expert"), None)
    return jax.shard_map(
        body,
        mesh=mesh,
        in_specs=(
            rows,
            rows,
            rows,
            rows,
            P("dp", "expert"),
            P("expert"),
            P("expert", None, None),
            P("expert", None, None),
        ),
        out_specs=(rows, rows, rows),
        check_vma=False,
    )
```

```python
import functools

import jax
import jax.numpy as jnp
from jax import lax
from jax.experimental import pallas as pl
from jax.experimental.pallas import tpu as pltpu
from jax.sharding import PartitionSpec as P

TOPK = 8
OVF = 16
MEMBERS = 16
TOK = 16
PARTS = 4
ROWS = MEMBERS * TOK
HALF = ROWS // 2
TILE = 256
CHUNK = 32
LANES = 128
MESH = pl.DeviceIdType.MESH

ORDER = [[(q + s) % 4 for s in range(4)] for q in range(PARTS)]


def slot_of(q, p):
    return sum(1 << ORDER[q][s] for s in range(4) if p >> s & 1)


PLACE = [{slot_of(q, p): p for p in range(MEMBERS)} for q in range(PARTS)]
SLOT = [[slot_of(q, p) for p in range(MEMBERS)] for q in range(PARTS)]
STEP_AT = [0, 128, 192, 224]
STEP_ROWS = [128, 64, 32, 16]


def flip(v, bits):
    if bits & 2:
        v = 3 - v
    if bits & 1:
        v = v + 1 - 2 * lax.rem(v, 2)
    return v


def recode(v):
    return v ^ ((v >> 1) & 5)


def nt_dot(a, b):
    return lax.dot_general(a, b, (((1,), (1,)), ((), ())), preferred_element_type=jnp.float32)


def nn_dot(a, b):
    return jnp.dot(a, b, preferred_element_type=jnp.float32)


def kernel(
    levels,
    tokens,
    grads,
    gates,
    routes,
    capacity,
    pair_mask,
    gate_up,
    down,
    out_ref,
    igrad_ref,
    ggrad_ref,
    gu_v,
    dn_v,
    xb,
    sb,
    rb,
    acc,
    p2,
    p3,
    hid,
    dpre,
    ta,
    tb,
    gates_v,
    routes_v,
    cap_s,
    mask_s,
    gsend,
    grecv,
    gmat,
    gkeep,
    knear,
    gcol,
    gnear,
    ggacc,
    qsend,
    qrecv,
    dsend,
    drecv,
    local_sem,
    tiny_sem,
    weight_sem,
    ag_send,
    ag_recv,
    rs_send,
    rs_recv,
    g_send,
    g_recv,
    q_send,
    q_recv,
    d_send,
    d_recv,
    k_send,
    k_recv,
    ready,
):
    width = tokens.shape[1]
    part = width // PARTS
    hidden = down.shape[2]
    dp = lax.axis_index("dp")
    me = lax.axis_index("expert")
    mx, my = lax.div(me, 4), lax.rem(me, 4)

    def member(j):
        return (dp, flip(mx, j >> 2) * 4 + flip(my, j & 3))

    def bit(b):
        return lax.rem(lax.div(dp, 1 << b), 2)

    def partner(b):
        return (dp + (1 << b) * (1 - 2 * bit(b)), me)

    tiny = [
        pltpu.make_async_copy(routes, routes_v, tiny_sem.at[0]),
        pltpu.make_async_copy(gates, gates_v, tiny_sem.at[1]),
        pltpu.make_async_copy(capacity, cap_s, tiny_sem.at[2]),
        pltpu.make_async_copy(pair_mask, mask_s, tiny_sem.at[3]),
    ]
    for copy in tiny:
        copy.start()
    barrier = pltpu.get_barrier_semaphore()
    for j in range(1, MEMBERS):
        pl.semaphore_signal(barrier, inc=1, device_id=member(j), device_id_type=MESH)
    heard = MEMBERS - 1
    for b in range(levels):
        heard = heard + bit(b)

        @pl.when(bit(b) == 0)
        def _():
            pl.semaphore_signal(barrier, inc=1, device_id=partner(b), device_id_type=MESH)

    sources = (tokens, grads)
    local = []
    for a in range(2):
        for q in range(PARTS):
            copy = pltpu.make_async_copy(
                sources[a].at[:, q * part : (q + 1) * part],
                xb.at[a * PARTS + q, 0:TOK, :],
                local_sem.at[a * PARTS + q],
            )
            copy.start()
            local.append(copy)
    weights = []
    for i in range(PARTS):
        rows = slice(i * part, (i + 1) * part)
        weights.append(
            pltpu.make_async_copy(gate_up.at[0, rows, :], gu_v.at[rows, :], weight_sem.at[i])
        )
    for i in range(PARTS):
        rows = slice(i * part, (i + 1) * part)
        weights.append(
            pltpu.make_async_copy(down.at[0, rows, :], dn_v.at[rows, :], weight_sem.at[4 + i])
        )
    for copy in weights:
        copy.start()

    my_code = recode(me)
    lane = lax.broadcasted_iota(jnp.int32, (TOK, LANES), 1)
    sub = lax.broadcasted_iota(jnp.int32, (TOK, LANES), 0)
    slots = lax.broadcasted_iota(jnp.int32, (MEMBERS, TOK), 0)
    for copy in tiny:
        copy.wait()
    rel = recode(routes_v[...]) ^ my_code
    gate_values = gates_v[...].astype(jnp.float32)
    dense = jnp.zeros((MEMBERS, TOK), jnp.float32)
    for k in range(TOPK):
        dense += jnp.where(slots == rel[k : k + 1, :], gate_values[k : k + 1, :], 0.0)
    gmat[...] = jnp.zeros_like(gmat)
    gmat[:, 0:TOK] = dense
    for j in range(MEMBERS):
        gsend[j] = gmat[j : j + 1, :]

    pl.semaphore_wait(barrier, heard)
    for b in range(levels):

        @pl.when(bit(b) == 1)
        def _():
            pl.semaphore_signal(ready.at[b], inc=1, device_id=partner(b), device_id_type=MESH)


    def gather(a, q, s):
        n = a * PARTS + q
        held = TOK << s
        if s == 0:
            src = sources[a].at[:, q * part : (q + 1) * part]
        else:
            src = xb.at[n, 0:held, :]
        return pltpu.make_async_remote_copy(
            src_ref=src,
            dst_ref=xb.at[n, held : 2 * held, :],
            send_sem=ag_send.at[n * 4 + s],
            recv_sem=ag_recv.at[n * 4 + s],
            device_id=member(1 << ORDER[q][s]),
            device_id_type=MESH,
        )

    def small(src, dst, send, recv, index, slot, other):
        return pltpu.make_async_remote_copy(
            src_ref=src.at[index],
            dst_ref=dst.at[slot],
            send_sem=send.at[slot],
            recv_sem=recv.at[slot],
            device_id=other,
            device_id_type=MESH,
        )

    gates_to = [small(gsend, grecv, g_send, g_recv, j, j, member(j)) for j in range(1, MEMBERS)]
    spare_to = [small(dsend, drecv, d_send, d_recv, 0, b, partner(b)) for b in range(levels)]
    quot_to = [small(qsend, qrecv, q_send, q_recv, j, j, member(j)) for j in range(1, MEMBERS)]

    def step_on(a, s):
        for q in range(PARTS):
            gather(a, q, s - 1).wait_recv()
            gather(a, q, s).start()

    for copy in gates_to:
        copy.start()
    for a in range(2):
        for q in range(PARTS):
            gather(a, q, 0).start()
    for copy in local:
        copy.wait()
    step_on(0, 1)
    step_on(1, 1)

    gmat[0:1, :] = gsend[0]
    for j in range(1, MEMBERS):
        gates_to[j - 1].wait_recv()
        gmat[j : j + 1, :] = grecv[j]
    mat = gmat[...]
    named16 = jnp.where(mat > 0.0, 1.0, 0.0).astype(jnp.bfloat16)
    counts = nn_dot(named16, jnp.ones((LANES, LANES), jnp.bfloat16)).astype(jnp.bfloat16)
    load = nn_dot(jnp.ones((MEMBERS, MEMBERS), jnp.bfloat16), counts)
    cap = jnp.broadcast_to(cap_s[...].astype(jnp.float32), (1, LANES))
    taken = jnp.minimum(cap - jnp.minimum(load, cap), float(OVF))
    dsend[0] = taken[0:1, :]
    for b in range(levels):

        @pl.when(bit(b) == 1)
        def _():
            spare_to[b].start()

    for s in range(2, 4):
        step_on(0, s)
        step_on(1, s)
    big0 = lax.broadcasted_iota(jnp.int32, (LANES, LANES), 0)
    big1 = lax.broadcasted_iota(jnp.int32, (LANES, LANES), 1)
    ahead = jnp.where(big0 < big1, 1.0, 0.0).astype(jnp.bfloat16)
    within = nn_dot(named16, ahead)
    row_home = recode(lax.broadcasted_iota(jnp.int32, (MEMBERS, MEMBERS), 0) ^ my_code)
    col_home = recode(lax.broadcasted_iota(jnp.int32, (MEMBERS, MEMBERS), 1) ^ my_code)
    earlier = jnp.where(col_home < row_home, 1.0, 0.0).astype(jnp.bfloat16)
    position = within + nn_dot(earlier, counts)
    for q in range(PARTS):
        gather(0, q, 3).wait_recv()
    for copy in weights[:4]:
        copy.wait()

    def block(a, q):
        pieces = []
        for j in range(MEMBERS):
            p = PLACE[q][j]
            pieces.append(xb[a * PARTS + q, p * TOK : (p + 1) * TOK, :])
        return jnp.concatenate(pieces, axis=0)

    def forward_tile(n, carry):
        at = pl.multiple_of(n * TILE, TILE)
        up_at = pl.multiple_of(hidden + n * TILE, TILE)
        gate_pre = jnp.zeros((ROWS, TILE), jnp.float32)
        up_pre = jnp.zeros((ROWS, TILE), jnp.float32)
        for q in range(PARTS):
            lhs = block(0, q)
            rows = slice(q * part, (q + 1) * part)
            gate_pre += nn_dot(lhs, gu_v[rows, pl.ds(at, TILE)])
            up_pre += nn_dot(lhs, gu_v[rows, pl.ds(up_at, TILE)])
        ta[...] = gate_pre
        tb[...] = up_pre

        def rows_of(i, inner):
            rows = pl.ds(pl.multiple_of(i * CHUNK, CHUNK), CHUNK)
            a = ta[rows, :]
            b = tb[rows, :]
            sigma = jax.nn.sigmoid(a)
            swish = a * sigma
            both = swish * b
            cols = pl.ds(at, TILE)
            p2[rows, cols] = swish
            p3[rows, cols] = b * sigma * (1.0 + a * (1.0 - sigma))
            hid[rows, cols] = both.astype(jnp.bfloat16)
            return inner

        return lax.fori_loop(0, ROWS // CHUNK, rows_of, carry)

    lax.fori_loop(0, hidden // TILE, forward_tile, 0)

    def reduce(a, q, r):
        n = a * PARTS + q
        rows = slice(STEP_AT[r], STEP_AT[r] + STEP_ROWS[r])
        return pltpu.make_async_remote_copy(
            src_ref=sb.at[n, rows, :],
            dst_ref=rb.at[n, rows, :],
            send_sem=rs_send.at[n * 4 + r],
            recv_sem=rs_recv.at[n * 4 + r],
            device_id=member(1 << ORDER[q][3 - r]),
            device_id_type=MESH,
        )

    def permuted(ref, q):
        return jnp.concatenate(
            [ref[SLOT[q][p] * TOK : (SLOT[q][p] + 1) * TOK, :] for p in range(MEMBERS)], axis=0
        )

    def produce(a, q, ref, weight):
        n = a * PARTS + q
        tile = min(TILE, part)
        for c in range(part // tile):
            cols = slice(c * tile, (c + 1) * tile)
            rows = slice(q * part + c * tile, q * part + (c + 1) * tile)
            value = nt_dot(permuted(ref, q), weight[rows, :])
            sb[n, 0:HALF, cols] = value[HALF:, :].astype(jnp.bfloat16)
            acc[n, :, cols] = value[:HALF, :]
        reduce(a, q, 0).start()

    for copy in weights[4:]:
        copy.wait()
    for q in range(PARTS):
        produce(0, q, hid, dn_v)

    for q in range(PARTS):
        gather(1, q, 3).wait_recv()
    ggacc[...] = jnp.zeros_like(ggacc)

    def backward_tile(n, carry):
        at = pl.multiple_of(n * TILE, TILE)
        up_at = pl.multiple_of(hidden + n * TILE, TILE)
        total = jnp.zeros((ROWS, TILE), jnp.float32)
        for q in range(PARTS):
            total += nn_dot(block(1, q), dn_v[q * part : (q + 1) * part, pl.ds(at, TILE)])
        ta[...] = total

        def rows_of(i, inner):
            rows = pl.ds(pl.multiple_of(i * CHUNK, CHUNK), CHUNK)
            cols = pl.ds(at, TILE)
            back = ta[rows, :]
            terms = back * hid[rows, cols].astype(jnp.float32)
            ggacc[rows, :] += terms[:, :LANES] + terms[:, LANES:]
            dpre[rows, cols] = (back * p3[rows, cols]).astype(jnp.bfloat16)
            dpre[rows, pl.ds(up_at, TILE)] = (back * p2[rows, cols]).astype(jnp.bfloat16)
            return inner

        return lax.fori_loop(0, ROWS // CHUNK, rows_of, carry)

    lax.fori_loop(0, hidden // TILE, backward_tile, 0)

    for q in range(PARTS):
        produce(1, q, dpre, gu_v)

    for b in range(levels):

        @pl.when(bit(b) == 0)
        def _():
            pl.semaphore_wait(ready.at[b], 1)
            spare_to[b].start()

    limit = cap
    for b in range(levels):
        spare_to[b].wait_recv()
        limit += drecv[b] * (mask_s[...] == 1 << b).astype(jnp.float32)
    gkeep[...] = jnp.where(position < limit, mat, 0.0)
    near_to = [
        pltpu.make_async_remote_copy(
            src_ref=gkeep,
            dst_ref=knear.at[i],
            send_sem=k_send.at[i],
            recv_sem=k_recv.at[i],
            device_id=member(1 << i),
            device_id_type=MESH,
        )
        for i in range(4)
    ]
    for copy in near_to:
        copy.start()

    def spread(row):
        row = jnp.broadcast_to(row, (TOK, LANES))
        column = jnp.sum(jnp.where(lane == sub, row, 0.0), axis=1, keepdims=True)
        return jnp.broadcast_to(column, (TOK, LANES))

    for j in range(MEMBERS):
        gcol[j * TOK : (j + 1) * TOK, :] = spread(gkeep[j : j + 1, :])
    for i in range(4):
        near_to[i].wait_recv()
        for j in range(MEMBERS):
            if not j >> i & 1:
                other = j ^ (1 << i)
                gnear[i, j * TOK : (j + 1) * TOK, :] = spread(knear[i, other : other + 1, :])

    def widen(rows):
        return jnp.concatenate([jnp.concatenate(rows, axis=0)] * (part // LANES), axis=1)

    def gate_rows(q, first, count):
        slots_in = [SLOT[q][p] * TOK for p in range(first, first + count)]
        return widen([gcol[at : at + TOK, :] for at in slots_in])

    def near_rows(q, first, count):
        slots_in = [SLOT[q][p] * TOK for p in range(first, first + count)]
        return widen([gnear[ORDER[q][3], at : at + TOK, :] for at in slots_in])

    def total_of(n, q, first, count, steps):
        size = count * TOK
        at = first * TOK
        total = acc[n, at : at + size, :] * gate_rows(q, first, count)
        for i in range(steps):
            term = rb[n, STEP_AT[i] + at : STEP_AT[i] + at + size, :].astype(jnp.float32)
            total += term * near_rows(q, first, count) if i == 0 else term
        return total.astype(jnp.bfloat16)

    def pass_on(a, q, r):
        n = a * PARTS + q
        reduce(a, q, r - 1).wait_recv()
        size = STEP_ROWS[r]
        count = size // TOK
        sb[n, STEP_AT[r] : STEP_AT[r] + size, :] = total_of(n, q, count, count, r)
        reduce(a, q, r).start()

    def finish(a, q, ref):
        n = a * PARTS + q
        reduce(a, q, 3).wait_recv()
        ref[:, q * part : (q + 1) * part] = total_of(n, q, 0, 1, 4)

    for q in range(PARTS):
        pass_on(0, q, 1)
    for q in range(PARTS):
        pass_on(1, q, 1)

    for j in range(MEMBERS):
        column = jnp.sum(ggacc[j * TOK : (j + 1) * TOK, :], axis=1, keepdims=True)
        row = jnp.sum(jnp.where(lane == sub, column, 0.0), axis=0, keepdims=True)
        qsend[j] = jnp.where(gkeep[j : j + 1, :] > 0.0, row, 0.0)
    for copy in quot_to:
        copy.start()

    for r in range(2, 4):
        for q in range(PARTS):
            pass_on(0, q, r)
        for q in range(PARTS):
            pass_on(1, q, r)

    gmat[0:1, :] = qsend[0]
    for j in range(1, MEMBERS):
        quot_to[j - 1].wait_recv()
        gmat[j : j + 1, :] = qrecv[j]
    by_slot = gmat[:, 0:TOK]
    for k in range(TOPK):
        ggrad_ref[k : k + 1, :] = jnp.sum(
            jnp.where(slots == rel[k : k + 1, :], by_slot, 0.0), axis=0, keepdims=True
        )

    for q in range(PARTS):
        finish(0, q, out_ref)
    for q in range(PARTS):
        finish(1, q, igrad_ref)

    for a in range(2):
        for q in range(PARTS):
            for s in range(4):
                gather(a, q, s).wait_send()
                reduce(a, q, s).wait_send()
    for copy in gates_to + spare_to + quot_to + near_to:
        copy.wait_send()


def body(tokens, grad_out, gate_probs, routes, capacity, pair_mask, gate_up_weight, down_weight):
    width = tokens.shape[1]
    hidden = down_weight.shape[2]
    part = width // PARTS
    levels = lax.axis_size("dp").bit_length() - 1
    vmem = pl.BlockSpec(memory_space=pltpu.VMEM)
    in_hbm = pl.BlockSpec(memory_space=pltpu.HBM)
    f32, b16 = jnp.float32, jnp.bfloat16
    dma = pltpu.SemaphoreType.DMA
    streams = 2 * PARTS
    out, igrad, ggrad = pl.pallas_call(
        functools.partial(kernel, levels),
        out_shape=(
            jax.ShapeDtypeStruct((TOK, width), b16),
            jax.ShapeDtypeStruct((TOK, width), b16),
            jax.ShapeDtypeStruct((TOPK, TOK), f32),
        ),
        in_specs=[in_hbm] * 8,
        out_specs=(vmem, vmem, vmem),
        scratch_shapes=[
            pltpu.VMEM((width, 2 * hidden), b16),
            pltpu.VMEM((width, hidden), b16),
            pltpu.VMEM((streams, ROWS, part), b16),
            pltpu.VMEM((streams, 240, part), b16),
            pltpu.VMEM((streams, 240, part), b16),
            pltpu.VMEM((streams, HALF, part), f32),
            pltpu.VMEM((ROWS, hidden), f32),
            pltpu.VMEM((ROWS, hidden), f32),
            pltpu.VMEM((ROWS, hidden), b16),
            pltpu.VMEM((ROWS, 2 * hidden), b16),
            pltpu.VMEM((ROWS, TILE), f32),
            pltpu.VMEM((ROWS, TILE), f32),
            pltpu.VMEM((TOPK, TOK), b16),
            pltpu.VMEM((TOPK, TOK), jnp.int32),
            pltpu.VMEM((1, 1), jnp.int32),
            pltpu.VMEM((1, 1), jnp.int32),
            pltpu.VMEM((MEMBERS, 1, LANES), f32),
            pltpu.VMEM((MEMBERS, 1, LANES), f32),
            pltpu.VMEM((MEMBERS, LANES), f32),
            pltpu.VMEM((MEMBERS, LANES), f32),
            pltpu.VMEM((4, MEMBERS, LANES), f32),
            pltpu.VMEM((ROWS, LANES), f32),
            pltpu.VMEM((4, ROWS, LANES), f32),
            pltpu.VMEM((ROWS, LANES), f32),
            pltpu.VMEM((MEMBERS, 1, LANES), f32),
            pltpu.VMEM((MEMBERS, 1, LANES), f32),
            pltpu.VMEM((1, 1, LANES), f32),
            pltpu.VMEM((16, 1, LANES), f32),
            dma((streams,)),
            dma((4,)),
            dma((8,)),
            dma((streams * 4,)),
            dma((streams * 4,)),
            dma((streams * 4,)),
            dma((streams * 4,)),
            dma((MEMBERS,)),
            dma((MEMBERS,)),
            dma((MEMBERS,)),
            dma((MEMBERS,)),
            dma((16,)),
            dma((16,)),
            dma((4,)),
            dma((4,)),
            pltpu.SemaphoreType.REGULAR((max(levels, 1),)),
        ],
        compiler_params=pltpu.CompilerParams(
            collective_id=0, has_side_effects=True, vmem_limit_bytes=60 * 1024 * 1024
        ),
        cost_estimate=pl.CostEstimate(
            flops=2 * ROWS * width * hidden * 6,
            bytes_accessed=width * hidden * 6,
            transcendentals=ROWS * hidden,
        ),
    )(
        tokens,
        grad_out,
        gate_probs.T,
        routes.T,
        capacity,
        pair_mask.reshape(1, 1),
        gate_up_weight,
        down_weight,
    )
    return (out, igrad, ggrad.T)


def solution(mesh):
    rows = P(("dp", "expert"), None)
    return jax.shard_map(
        body,
        mesh=mesh,
        in_specs=(
            rows,
            rows,
            rows,
            rows,
            P("dp", "expert"),
            P("expert"),
            P("expert", None, None),
            P("expert", None, None),
        ),
        out_specs=(rows, rows, rows),
        check_vma=False,
    )
```

```python
import functools

import jax
import jax.numpy as jnp
from jax import lax
from jax.experimental import pallas as pl
from jax.experimental.pallas import tpu as pltpu
from jax.sharding import PartitionSpec as P

TOPK = 8
OVF = 16
MEMBERS = 16
TOK = 16
PARTS = 4
ROWS = MEMBERS * TOK
HALF = ROWS // 2
TILE = 256
CHUNK = 32
LANES = 128
MESH = pl.DeviceIdType.MESH

ORDER = [[(q + s) % 4 for s in range(4)] for q in range(PARTS)]


def slot_of(q, p):
    return sum(1 << ORDER[q][s] for s in range(4) if p >> s & 1)


PLACE = [{slot_of(q, p): p for p in range(MEMBERS)} for q in range(PARTS)]
SLOT = [[slot_of(q, p) for p in range(MEMBERS)] for q in range(PARTS)]
STEP_AT = [0, 128, 192, 224]
STEP_ROWS = [128, 64, 32, 16]


def flip(v, bits):
    if bits & 2:
        v = 3 - v
    if bits & 1:
        v = v + 1 - 2 * lax.rem(v, 2)
    return v


def recode(v):
    return v ^ ((v >> 1) & 5)


def nt_dot(a, b):
    return lax.dot_general(a, b, (((1,), (1,)), ((), ())), preferred_element_type=jnp.float32)


def nn_dot(a, b):
    return jnp.dot(a, b, preferred_element_type=jnp.float32)


def kernel(
    levels,
    tokens,
    grads,
    gates,
    routes,
    capacity,
    pair_mask,
    gate_up,
    down,
    out_ref,
    igrad_ref,
    ggrad_ref,
    gu_v,
    dn_v,
    xb,
    sb,
    rb,
    acc,
    p2,
    p3,
    hid,
    dpre,
    ta,
    tb,
    gates_v,
    routes_v,
    cap_s,
    mask_s,
    gsend,
    grecv,
    gmat,
    gkeep,
    gpos,
    knear,
    gcol,
    gnear,
    pcol,
    pnear,
    lsend,
    lnear,
    qrow,
    ggacc,
    qsend,
    qrecv,
    dsend,
    drecv,
    local_sem,
    tiny_sem,
    weight_sem,
    ag_send,
    ag_recv,
    rs_send,
    rs_recv,
    g_send,
    g_recv,
    q_send,
    q_recv,
    d_send,
    d_recv,
    k_send,
    k_recv,
    l_send,
    l_recv,
    ready,
):
    width = tokens.shape[1]
    part = width // PARTS
    hidden = down.shape[2]
    dp = lax.axis_index("dp")
    me = lax.axis_index("expert")
    mx, my = lax.div(me, 4), lax.rem(me, 4)

    def member(j):
        return (dp, flip(mx, j >> 2) * 4 + flip(my, j & 3))

    def bit(b):
        return lax.rem(lax.div(dp, 1 << b), 2)

    def partner(b):
        return (dp + (1 << b) * (1 - 2 * bit(b)), me)

    tiny = [
        pltpu.make_async_copy(routes, routes_v, tiny_sem.at[0]),
        pltpu.make_async_copy(gates, gates_v, tiny_sem.at[1]),
        pltpu.make_async_copy(capacity, cap_s, tiny_sem.at[2]),
        pltpu.make_async_copy(pair_mask, mask_s, tiny_sem.at[3]),
    ]
    for copy in tiny:
        copy.start()
    barrier = pltpu.get_barrier_semaphore()
    for j in range(1, MEMBERS):
        pl.semaphore_signal(barrier, inc=1, device_id=member(j), device_id_type=MESH)
    heard = MEMBERS - 1
    for b in range(levels):
        heard = heard + bit(b)

        @pl.when(bit(b) == 0)
        def _():
            pl.semaphore_signal(barrier, inc=1, device_id=partner(b), device_id_type=MESH)

    sources = (tokens, grads)
    local = []
    for a in range(2):
        for q in range(PARTS):
            copy = pltpu.make_async_copy(
                sources[a].at[:, q * part : (q + 1) * part],
                xb.at[a * PARTS + q, 0:TOK, :],
                local_sem.at[a * PARTS + q],
            )
            copy.start()
            local.append(copy)
    weights = []
    for i in range(PARTS):
        rows = slice(i * part, (i + 1) * part)
        weights.append(
            pltpu.make_async_copy(gate_up.at[0, rows, :], gu_v.at[rows, :], weight_sem.at[i])
        )
    for i in range(PARTS):
        rows = slice(i * part, (i + 1) * part)
        weights.append(
            pltpu.make_async_copy(down.at[0, rows, :], dn_v.at[rows, :], weight_sem.at[4 + i])
        )
    for copy in weights:
        copy.start()

    my_code = recode(me)
    lane = lax.broadcasted_iota(jnp.int32, (TOK, LANES), 1)
    sub = lax.broadcasted_iota(jnp.int32, (TOK, LANES), 0)
    slots = lax.broadcasted_iota(jnp.int32, (MEMBERS, TOK), 0)
    for copy in tiny:
        copy.wait()
    rel = recode(routes_v[...]) ^ my_code
    gate_values = gates_v[...].astype(jnp.float32)
    dense = jnp.zeros((MEMBERS, TOK), jnp.float32)
    for k in range(TOPK):
        dense += jnp.where(slots == rel[k : k + 1, :], gate_values[k : k + 1, :], 0.0)
    gmat[...] = jnp.zeros_like(gmat)
    gmat[:, 0:TOK] = dense
    for j in range(MEMBERS):
        gsend[j] = gmat[j : j + 1, :]

    pl.semaphore_wait(barrier, heard)
    for b in range(levels):

        @pl.when(bit(b) == 1)
        def _():
            pl.semaphore_signal(ready.at[b], inc=1, device_id=partner(b), device_id_type=MESH)


    def gather(a, q, s):
        n = a * PARTS + q
        held = TOK << s
        if s == 0:
            src = sources[a].at[:, q * part : (q + 1) * part]
        else:
            src = xb.at[n, 0:held, :]
        return pltpu.make_async_remote_copy(
            src_ref=src,
            dst_ref=xb.at[n, held : 2 * held, :],
            send_sem=ag_send.at[n * 4 + s],
            recv_sem=ag_recv.at[n * 4 + s],
            device_id=member(1 << ORDER[q][s]),
            device_id_type=MESH,
        )

    def small(src, dst, send, recv, index, slot, other):
        return pltpu.make_async_remote_copy(
            src_ref=src.at[index],
            dst_ref=dst.at[slot],
            send_sem=send.at[slot],
            recv_sem=recv.at[slot],
            device_id=other,
            device_id_type=MESH,
        )

    def near(src, dst, send, recv, i):
        return pltpu.make_async_remote_copy(
            src_ref=src,
            dst_ref=dst,
            send_sem=send.at[i],
            recv_sem=recv.at[i],
            device_id=member(1 << i),
            device_id_type=MESH,
        )

    gates_to = [small(gsend, grecv, g_send, g_recv, j, j, member(j)) for j in range(1, MEMBERS)]
    spare_to = [small(dsend, drecv, d_send, d_recv, 0, b, partner(b)) for b in range(levels)]
    quot_to = [small(qsend, qrecv, q_send, q_recv, j, j, member(j)) for j in range(1, MEMBERS)]

    def step_on(a, s):
        for q in range(PARTS):
            gather(a, q, s - 1).wait_recv()
            gather(a, q, s).start()

    for copy in gates_to:
        copy.start()
    for a in range(2):
        for q in range(PARTS):
            gather(a, q, 0).start()
    for copy in local:
        copy.wait()
    step_on(0, 1)
    step_on(1, 1)

    gmat[0:1, :] = gsend[0]
    for j in range(1, MEMBERS):
        gates_to[j - 1].wait_recv()
        gmat[j : j + 1, :] = grecv[j]
    mat = gmat[...]
    named16 = jnp.where(mat > 0.0, 1.0, 0.0).astype(jnp.bfloat16)
    counts = nn_dot(named16, jnp.ones((LANES, LANES), jnp.bfloat16)).astype(jnp.bfloat16)
    load = nn_dot(jnp.ones((MEMBERS, MEMBERS), jnp.bfloat16), counts)
    cap = jnp.broadcast_to(cap_s[...].astype(jnp.float32), (1, LANES))
    taken = jnp.minimum(cap - jnp.minimum(load, cap), float(OVF))
    dsend[0] = taken[0:1, :]
    for b in range(levels):

        @pl.when(bit(b) == 1)
        def _():
            spare_to[b].start()

    for s in range(2, 4):
        step_on(0, s)
        step_on(1, s)
    big0 = lax.broadcasted_iota(jnp.int32, (LANES, LANES), 0)
    big1 = lax.broadcasted_iota(jnp.int32, (LANES, LANES), 1)
    ahead = jnp.where(big0 < big1, 1.0, 0.0).astype(jnp.bfloat16)
    within = nn_dot(named16, ahead)
    row_home = recode(lax.broadcasted_iota(jnp.int32, (MEMBERS, MEMBERS), 0) ^ my_code)
    col_home = recode(lax.broadcasted_iota(jnp.int32, (MEMBERS, MEMBERS), 1) ^ my_code)
    earlier = jnp.where(col_home < row_home, 1.0, 0.0).astype(jnp.bfloat16)
    position = within + nn_dot(earlier, counts)
    gpos[0:MEMBERS, :] = mat
    gpos[MEMBERS : 2 * MEMBERS, :] = position
    near_to = [near(gpos, knear.at[i], k_send, k_recv, i) for i in range(4)]
    for copy in near_to:
        copy.start()
    for q in range(PARTS):
        gather(0, q, 3).wait_recv()
    for copy in weights[:4]:
        copy.wait()

    def block(a, q):
        pieces = []
        for j in range(MEMBERS):
            p = PLACE[q][j]
            pieces.append(xb[a * PARTS + q, p * TOK : (p + 1) * TOK, :])
        return jnp.concatenate(pieces, axis=0)

    def forward_tile(n, carry):
        at = pl.multiple_of(n * TILE, TILE)
        up_at = pl.multiple_of(hidden + n * TILE, TILE)
        gate_pre = jnp.zeros((ROWS, TILE), jnp.float32)
        up_pre = jnp.zeros((ROWS, TILE), jnp.float32)
        for q in range(PARTS):
            lhs = block(0, q)
            rows = slice(q * part, (q + 1) * part)
            gate_pre += nn_dot(lhs, gu_v[rows, pl.ds(at, TILE)])
            up_pre += nn_dot(lhs, gu_v[rows, pl.ds(up_at, TILE)])
        ta[...] = gate_pre
        tb[...] = up_pre

        def rows_of(i, inner):
            rows = pl.ds(pl.multiple_of(i * CHUNK, CHUNK), CHUNK)
            a = ta[rows, :]
            b = tb[rows, :]
            sigma = jax.nn.sigmoid(a)
            swish = a * sigma
            both = swish * b
            cols = pl.ds(at, TILE)
            p2[rows, cols] = swish
            p3[rows, cols] = b * sigma * (1.0 + a * (1.0 - sigma))
            hid[rows, cols] = both.astype(jnp.bfloat16)
            return inner

        return lax.fori_loop(0, ROWS // CHUNK, rows_of, carry)

    lax.fori_loop(0, hidden // TILE, forward_tile, 0)

    def reduce(a, q, r):
        n = a * PARTS + q
        rows = slice(STEP_AT[r], STEP_AT[r] + STEP_ROWS[r])
        return pltpu.make_async_remote_copy(
            src_ref=sb.at[n, rows, :],
            dst_ref=rb.at[n, rows, :],
            send_sem=rs_send.at[n * 4 + r],
            recv_sem=rs_recv.at[n * 4 + r],
            device_id=member(1 << ORDER[q][3 - r]),
            device_id_type=MESH,
        )

    def permuted(ref, q):
        return jnp.concatenate(
            [ref[SLOT[q][p] * TOK : (SLOT[q][p] + 1) * TOK, :] for p in range(MEMBERS)], axis=0
        )

    def produce(a, q, ref, weight):
        n = a * PARTS + q
        tile = min(TILE, part)
        for c in range(part // tile):
            cols = slice(c * tile, (c + 1) * tile)
            rows = slice(q * part + c * tile, q * part + (c + 1) * tile)
            value = nt_dot(permuted(ref, q), weight[rows, :])
            sb[n, 0:HALF, cols] = value[HALF:, :].astype(jnp.bfloat16)
            acc[n, :, cols] = value[:HALF, :]
        reduce(a, q, 0).start()

    for copy in weights[4:]:
        copy.wait()
    for q in range(PARTS):
        produce(0, q, hid, dn_v)

    for q in range(PARTS):
        gather(1, q, 3).wait_recv()
    ggacc[...] = jnp.zeros_like(ggacc)

    def backward_tile(n, carry):
        at = pl.multiple_of(n * TILE, TILE)
        up_at = pl.multiple_of(hidden + n * TILE, TILE)
        total = jnp.zeros((ROWS, TILE), jnp.float32)
        for q in range(PARTS):
            total += nn_dot(block(1, q), dn_v[q * part : (q + 1) * part, pl.ds(at, TILE)])
        ta[...] = total

        def rows_of(i, inner):
            rows = pl.ds(pl.multiple_of(i * CHUNK, CHUNK), CHUNK)
            cols = pl.ds(at, TILE)
            back = ta[rows, :]
            terms = back * hid[rows, cols].astype(jnp.float32)
            ggacc[rows, :] += terms[:, :LANES] + terms[:, LANES:]
            dpre[rows, cols] = (back * p3[rows, cols]).astype(jnp.bfloat16)
            dpre[rows, pl.ds(up_at, TILE)] = (back * p2[rows, cols]).astype(jnp.bfloat16)
            return inner

        return lax.fori_loop(0, ROWS // CHUNK, rows_of, carry)

    lax.fori_loop(0, hidden // TILE, backward_tile, 0)

    for q in range(PARTS):
        produce(1, q, dpre, gu_v)

    def spread(row):
        row = jnp.broadcast_to(row, (TOK, LANES))
        column = jnp.sum(jnp.where(lane == sub, row, 0.0), axis=1, keepdims=True)
        return jnp.broadcast_to(column, (TOK, LANES))

    for j in range(MEMBERS):
        rows = slice(j * TOK, (j + 1) * TOK)
        gcol[rows, :] = spread(gpos[j : j + 1, :])
        pcol[rows, :] = spread(gpos[MEMBERS + j : MEMBERS + j + 1, :])
        column = jnp.sum(ggacc[rows, :], axis=1, keepdims=True)
        qrow[j : j + 1, :] = jnp.sum(jnp.where(lane == sub, column, 0.0), axis=0, keepdims=True)
    for i in range(4):
        near_to[i].wait_recv()
        for j in range(MEMBERS):
            rows = slice(j * TOK, (j + 1) * TOK)
            other = j ^ (1 << i)
            if j >> i & 1:
                gnear[i, rows, :] = jnp.zeros((TOK, LANES), jnp.float32)
                pnear[i, rows, :] = jnp.zeros((TOK, LANES), jnp.float32)
            else:
                gnear[i, rows, :] = spread(knear[i, other : other + 1, :])
                pnear[i, rows, :] = spread(knear[i, MEMBERS + other : MEMBERS + other + 1, :])

    for b in range(levels):

        @pl.when(bit(b) == 0)
        def _():
            pl.semaphore_wait(ready.at[b], 1)
            spare_to[b].start()

    limit = cap
    for b in range(levels):
        spare_to[b].wait_recv()
        limit += drecv[b] * (mask_s[...] == 1 << b).astype(jnp.float32)
    lsend[0] = limit
    limits_to = [near(lsend.at[0], lnear.at[i], l_send, l_recv, i) for i in range(4)]
    for copy in limits_to:
        copy.start()
    gcol[...] = jnp.where(pcol[...] < limit, gcol[...], 0.0)
    kept = (mat > 0.0) & (position < limit)
    gkeep[...] = jnp.where(kept, qrow[...], 0.0)
    for j in range(MEMBERS):
        qsend[j] = gkeep[j : j + 1, :]
    for copy in quot_to:
        copy.start()
    for i in range(4):
        limits_to[i].wait_recv()
        gnear[i] = jnp.where(pnear[i] < lnear[i], gnear[i], 0.0)

    def widen(rows):
        return jnp.concatenate([jnp.concatenate(rows, axis=0)] * (part // LANES), axis=1)

    def gate_rows(q, first, count):
        slots_in = [SLOT[q][p] * TOK for p in range(first, first + count)]
        return widen([gcol[at : at + TOK, :] for at in slots_in])

    def near_rows(q, first, count):
        slots_in = [SLOT[q][p] * TOK for p in range(first, first + count)]
        return widen([gnear[ORDER[q][3], at : at + TOK, :] for at in slots_in])

    def total_of(n, q, first, count, steps):
        size = count * TOK
        at = first * TOK
        total = acc[n, at : at + size, :] * gate_rows(q, first, count)
        for i in range(steps):
            term = rb[n, STEP_AT[i] + at : STEP_AT[i] + at + size, :].astype(jnp.float32)
            total += term * near_rows(q, first, count) if i == 0 else term
        return total.astype(jnp.bfloat16)

    def pass_on(a, q, r):
        n = a * PARTS + q
        reduce(a, q, r - 1).wait_recv()
        size = STEP_ROWS[r]
        count = size // TOK
        sb[n, STEP_AT[r] : STEP_AT[r] + size, :] = total_of(n, q, count, count, r)
        reduce(a, q, r).start()

    def finish(a, q, ref):
        n = a * PARTS + q
        reduce(a, q, 3).wait_recv()
        ref[:, q * part : (q + 1) * part] = total_of(n, q, 0, 1, 4)

    for q in range(PARTS):
        pass_on(0, q, 1)
    for q in range(PARTS):
        pass_on(1, q, 1)

    for r in range(2, 4):
        for q in range(PARTS):
            pass_on(0, q, r)
        for q in range(PARTS):
            pass_on(1, q, r)

    gmat[0:1, :] = qsend[0]
    for j in range(1, MEMBERS):
        quot_to[j - 1].wait_recv()
        gmat[j : j + 1, :] = qrecv[j]
    by_slot = gmat[:, 0:TOK]
    for k in range(TOPK):
        ggrad_ref[k : k + 1, :] = jnp.sum(
            jnp.where(slots == rel[k : k + 1, :], by_slot, 0.0), axis=0, keepdims=True
        )

    for q in range(PARTS):
        finish(0, q, out_ref)
    for q in range(PARTS):
        finish(1, q, igrad_ref)

    for a in range(2):
        for q in range(PARTS):
            for s in range(4):
                gather(a, q, s).wait_send()
                reduce(a, q, s).wait_send()
    for copy in gates_to + spare_to + quot_to + near_to + limits_to:
        copy.wait_send()


def body(tokens, grad_out, gate_probs, routes, capacity, pair_mask, gate_up_weight, down_weight):
    width = tokens.shape[1]
    hidden = down_weight.shape[2]
    part = width // PARTS
    levels = lax.axis_size("dp").bit_length() - 1
    vmem = pl.BlockSpec(memory_space=pltpu.VMEM)
    in_hbm = pl.BlockSpec(memory_space=pltpu.HBM)
    f32, b16 = jnp.float32, jnp.bfloat16
    dma = pltpu.SemaphoreType.DMA
    streams = 2 * PARTS
    out, igrad, ggrad = pl.pallas_call(
        functools.partial(kernel, levels),
        out_shape=(
            jax.ShapeDtypeStruct((TOK, width), b16),
            jax.ShapeDtypeStruct((TOK, width), b16),
            jax.ShapeDtypeStruct((TOPK, TOK), f32),
        ),
        in_specs=[in_hbm] * 8,
        out_specs=(vmem, vmem, vmem),
        scratch_shapes=[
            pltpu.VMEM((width, 2 * hidden), b16),
            pltpu.VMEM((width, hidden), b16),
            pltpu.VMEM((streams, ROWS, part), b16),
            pltpu.VMEM((streams, 240, part), b16),
            pltpu.VMEM((streams, 240, part), b16),
            pltpu.VMEM((streams, HALF, part), f32),
            pltpu.VMEM((ROWS, hidden), f32),
            pltpu.VMEM((ROWS, hidden), f32),
            pltpu.VMEM((ROWS, hidden), b16),
            pltpu.VMEM((ROWS, 2 * hidden), b16),
            pltpu.VMEM((ROWS, TILE), f32),
            pltpu.VMEM((ROWS, TILE), f32),
            pltpu.VMEM((TOPK, TOK), b16),
            pltpu.VMEM((TOPK, TOK), jnp.int32),
            pltpu.VMEM((1, 1), jnp.int32),
            pltpu.VMEM((1, 1), jnp.int32),
            pltpu.VMEM((MEMBERS, 1, LANES), f32),
            pltpu.VMEM((MEMBERS, 1, LANES), f32),
            pltpu.VMEM((MEMBERS, LANES), f32),
            pltpu.VMEM((MEMBERS, LANES), f32),
            pltpu.VMEM((2 * MEMBERS, LANES), f32),
            pltpu.VMEM((4, 2 * MEMBERS, LANES), f32),
            pltpu.VMEM((ROWS, LANES), f32),
            pltpu.VMEM((4, ROWS, LANES), f32),
            pltpu.VMEM((ROWS, LANES), f32),
            pltpu.VMEM((4, ROWS, LANES), f32),
            pltpu.VMEM((1, 1, LANES), f32),
            pltpu.VMEM((4, 1, LANES), f32),
            pltpu.VMEM((MEMBERS, LANES), f32),
            pltpu.VMEM((ROWS, LANES), f32),
            pltpu.VMEM((MEMBERS, 1, LANES), f32),
            pltpu.VMEM((MEMBERS, 1, LANES), f32),
            pltpu.VMEM((1, 1, LANES), f32),
            pltpu.VMEM((16, 1, LANES), f32),
            dma((streams,)),
            dma((4,)),
            dma((8,)),
            dma((streams * 4,)),
            dma((streams * 4,)),
            dma((streams * 4,)),
            dma((streams * 4,)),
            dma((MEMBERS,)),
            dma((MEMBERS,)),
            dma((MEMBERS,)),
            dma((MEMBERS,)),
            dma((16,)),
            dma((16,)),
            dma((4,)),
            dma((4,)),
            dma((4,)),
            dma((4,)),
            pltpu.SemaphoreType.REGULAR((max(levels, 1),)),
        ],
        compiler_params=pltpu.CompilerParams(
            collective_id=0, has_side_effects=True, vmem_limit_bytes=60 * 1024 * 1024
        ),
        cost_estimate=pl.CostEstimate(
            flops=2 * ROWS * width * hidden * 6,
            bytes_accessed=width * hidden * 6,
            transcendentals=ROWS * hidden,
        ),
    )(
        tokens,
        grad_out,
        gate_probs.T,
        routes.T,
        capacity,
        pair_mask.reshape(1, 1),
        gate_up_weight,
        down_weight,
    )
    return (out, igrad, ggrad.T)


def solution(mesh):
    rows = P(("dp", "expert"), None)
    return jax.shard_map(
        body,
        mesh=mesh,
        in_specs=(
            rows,
            rows,
            rows,
            rows,
            P("dp", "expert"),
            P("expert"),
            P("expert", None, None),
            P("expert", None, None),
        ),
        out_specs=(rows, rows, rows),
        check_vma=False,
    )
```

```python
import functools

import jax
import jax.numpy as jnp
from jax import lax
from jax.experimental import pallas as pl
from jax.experimental.pallas import tpu as pltpu
from jax.sharding import PartitionSpec as P

TOPK = 8
OVF = 16
MEMBERS = 16
TOK = 16
PARTS = 4
ROWS = MEMBERS * TOK
HALF = ROWS // 2
TILE = 256
CHUNK = 32
LANES = 128
MESH = pl.DeviceIdType.MESH

ORDER = [[(q + s) % 4 for s in range(4)] for q in range(PARTS)]


def slot_of(q, p):
    return sum(1 << ORDER[q][s] for s in range(4) if p >> s & 1)


PLACE = [{slot_of(q, p): p for p in range(MEMBERS)} for q in range(PARTS)]
SLOT = [[slot_of(q, p) for p in range(MEMBERS)] for q in range(PARTS)]
STEP_AT = [0, 128, 192, 224]
STEP_ROWS = [128, 64, 32, 16]


def flip(v, bits):
    if bits & 2:
        v = 3 - v
    if bits & 1:
        v = v + 1 - 2 * lax.rem(v, 2)
    return v


def recode(v):
    return v ^ ((v >> 1) & 5)


def nt_dot(a, b):
    return lax.dot_general(a, b, (((1,), (1,)), ((), ())), preferred_element_type=jnp.float32)


def nn_dot(a, b):
    return jnp.dot(a, b, preferred_element_type=jnp.float32)


def kernel(
    levels,
    tokens,
    grads,
    gates,
    routes,
    capacity,
    pair_mask,
    gate_up,
    down,
    out_ref,
    igrad_ref,
    ggrad_ref,
    gu_v,
    dn_v,
    xb,
    sb,
    rb,
    acc,
    p2,
    p3,
    hid,
    dpre,
    ta,
    tb,
    gates_v,
    routes_v,
    cap_s,
    mask_s,
    gsend,
    grecv,
    gmat,
    gkeep,
    gpos,
    knear,
    gcol,
    gnear,
    pcol,
    pnear,
    lsend,
    lnear,
    qrow,
    ggacc,
    qsend,
    qrecv,
    dsend,
    drecv,
    local_sem,
    tiny_sem,
    weight_sem,
    ag_send,
    ag_recv,
    rs_send,
    rs_recv,
    g_send,
    g_recv,
    q_send,
    q_recv,
    d_send,
    d_recv,
    k_send,
    k_recv,
    l_send,
    l_recv,
    ready,
):
    width = tokens.shape[1]
    part = width // PARTS
    hidden = down.shape[2]
    dp = lax.axis_index("dp")
    me = lax.axis_index("expert")
    mx, my = lax.div(me, 4), lax.rem(me, 4)

    def member(j):
        return (dp, flip(mx, j >> 2) * 4 + flip(my, j & 3))

    def bit(b):
        return lax.rem(lax.div(dp, 1 << b), 2)

    def partner(b):
        return (dp + (1 << b) * (1 - 2 * bit(b)), me)

    tiny = [
        pltpu.make_async_copy(routes, routes_v, tiny_sem.at[0]),
        pltpu.make_async_copy(gates, gates_v, tiny_sem.at[1]),
        pltpu.make_async_copy(capacity, cap_s, tiny_sem.at[2]),
        pltpu.make_async_copy(pair_mask, mask_s, tiny_sem.at[3]),
    ]
    for copy in tiny:
        copy.start()
    barrier = pltpu.get_barrier_semaphore()
    for j in range(1, MEMBERS):
        pl.semaphore_signal(barrier, inc=1, device_id=member(j), device_id_type=MESH)
    heard = MEMBERS - 1
    for b in range(levels):
        heard = heard + bit(b)

        @pl.when(bit(b) == 0)
        def _():
            pl.semaphore_signal(barrier, inc=1, device_id=partner(b), device_id_type=MESH)

    sources = (tokens, grads)
    local = []
    for a in range(2):
        for q in range(PARTS):
            copy = pltpu.make_async_copy(
                sources[a].at[:, q * part : (q + 1) * part],
                xb.at[a * PARTS + q, 0:TOK, :],
                local_sem.at[a * PARTS + q],
            )
            copy.start()
            local.append(copy)
    weights = []
    for i in range(PARTS):
        rows = slice(i * part, (i + 1) * part)
        weights.append(
            pltpu.make_async_copy(gate_up.at[0, rows, :], gu_v.at[rows, :], weight_sem.at[i])
        )
    for i in range(PARTS):
        rows = slice(i * part, (i + 1) * part)
        weights.append(
            pltpu.make_async_copy(down.at[0, rows, :], dn_v.at[rows, :], weight_sem.at[4 + i])
        )
    for copy in weights:
        copy.start()

    my_code = recode(me)
    lane = lax.broadcasted_iota(jnp.int32, (TOK, LANES), 1)
    sub = lax.broadcasted_iota(jnp.int32, (TOK, LANES), 0)
    slots = lax.broadcasted_iota(jnp.int32, (MEMBERS, TOK), 0)
    for copy in tiny:
        copy.wait()
    rel = recode(routes_v[...]) ^ my_code
    gate_values = gates_v[...].astype(jnp.float32)
    dense = jnp.zeros((MEMBERS, TOK), jnp.float32)
    for k in range(TOPK):
        dense += jnp.where(slots == rel[k : k + 1, :], gate_values[k : k + 1, :], 0.0)
    gmat[...] = jnp.zeros_like(gmat)
    gmat[:, 0:TOK] = dense
    for j in range(MEMBERS):
        gsend[j] = gmat[j : j + 1, :]

    pl.semaphore_wait(barrier, heard)
    for b in range(levels):

        @pl.when(bit(b) == 1)
        def _():
            pl.semaphore_signal(ready.at[b], inc=1, device_id=partner(b), device_id_type=MESH)


    def gather(a, q, s):
        n = a * PARTS + q
        held = TOK << s
        if s == 0:
            src = sources[a].at[:, q * part : (q + 1) * part]
        else:
            src = xb.at[n, 0:held, :]
        return pltpu.make_async_remote_copy(
            src_ref=src,
            dst_ref=xb.at[n, held : 2 * held, :],
            send_sem=ag_send.at[n * 4 + s],
            recv_sem=ag_recv.at[n * 4 + s],
            device_id=member(1 << ORDER[q][s]),
            device_id_type=MESH,
        )

    def small(src, dst, send, recv, index, slot, other):
        return pltpu.make_async_remote_copy(
            src_ref=src.at[index],
            dst_ref=dst.at[slot],
            send_sem=send.at[slot],
            recv_sem=recv.at[slot],
            device_id=other,
            device_id_type=MESH,
        )

    def near(src, dst, send, recv, i):
        return pltpu.make_async_remote_copy(
            src_ref=src,
            dst_ref=dst,
            send_sem=send.at[i],
            recv_sem=recv.at[i],
            device_id=member(1 << i),
            device_id_type=MESH,
        )

    gates_to = [small(gsend, grecv, g_send, g_recv, j, j, member(j)) for j in range(1, MEMBERS)]
    spare_to = [small(dsend, drecv, d_send, d_recv, 0, b, partner(b)) for b in range(levels)]
    quot_to = [small(qsend, qrecv, q_send, q_recv, j, j, member(j)) for j in range(1, MEMBERS)]

    def step_on(a, s):
        for q in range(PARTS):
            gather(a, q, s - 1).wait_recv()
            gather(a, q, s).start()

    for a in range(2):
        for q in range(PARTS):
            gather(a, q, 0).start()
    for copy in gates_to:
        copy.start()
    for copy in local:
        copy.wait()
    for s in range(1, 3):
        step_on(0, s)
        step_on(1, s)

    gmat[0:1, :] = gsend[0]
    for j in range(1, MEMBERS):
        gates_to[j - 1].wait_recv()
        gmat[j : j + 1, :] = grecv[j]
    mat = gmat[...]
    named16 = jnp.where(mat > 0.0, 1.0, 0.0).astype(jnp.bfloat16)
    counts = nn_dot(named16, jnp.ones((LANES, LANES), jnp.bfloat16)).astype(jnp.bfloat16)
    load = nn_dot(jnp.ones((MEMBERS, MEMBERS), jnp.bfloat16), counts)
    cap = jnp.broadcast_to(cap_s[...].astype(jnp.float32), (1, LANES))
    taken = jnp.minimum(cap - jnp.minimum(load, cap), float(OVF))
    dsend[0] = taken[0:1, :]
    for b in range(levels):

        @pl.when(bit(b) == 1)
        def _():
            spare_to[b].start()

    step_on(0, 3)
    step_on(1, 3)
    big0 = lax.broadcasted_iota(jnp.int32, (LANES, LANES), 0)
    big1 = lax.broadcasted_iota(jnp.int32, (LANES, LANES), 1)
    ahead = jnp.where(big0 < big1, 1.0, 0.0).astype(jnp.bfloat16)
    within = nn_dot(named16, ahead)
    row_home = recode(lax.broadcasted_iota(jnp.int32, (MEMBERS, MEMBERS), 0) ^ my_code)
    col_home = recode(lax.broadcasted_iota(jnp.int32, (MEMBERS, MEMBERS), 1) ^ my_code)
    earlier = jnp.where(col_home < row_home, 1.0, 0.0).astype(jnp.bfloat16)
    position = within + nn_dot(earlier, counts)
    gpos[0:MEMBERS, :] = mat
    gpos[MEMBERS : 2 * MEMBERS, :] = position
    near_to = [near(gpos, knear.at[i], k_send, k_recv, i) for i in range(4)]
    for copy in near_to:
        copy.start()
    for q in range(PARTS):
        gather(0, q, 3).wait_recv()
    for copy in weights[:4]:
        copy.wait()

    def block(a, q):
        pieces = []
        for j in range(MEMBERS):
            p = PLACE[q][j]
            pieces.append(xb[a * PARTS + q, p * TOK : (p + 1) * TOK, :])
        return jnp.concatenate(pieces, axis=0)

    def forward_tile(n, carry):
        at = pl.multiple_of(n * TILE, TILE)
        up_at = pl.multiple_of(hidden + n * TILE, TILE)
        gate_pre = jnp.zeros((ROWS, TILE), jnp.float32)
        up_pre = jnp.zeros((ROWS, TILE), jnp.float32)
        for q in range(PARTS):
            lhs = block(0, q)
            rows = slice(q * part, (q + 1) * part)
            gate_pre += nn_dot(lhs, gu_v[rows, pl.ds(at, TILE)])
            up_pre += nn_dot(lhs, gu_v[rows, pl.ds(up_at, TILE)])
        ta[...] = gate_pre
        tb[...] = up_pre

        def rows_of(i, inner):
            rows = pl.ds(pl.multiple_of(i * CHUNK, CHUNK), CHUNK)
            a = ta[rows, :]
            b = tb[rows, :]
            sigma = jax.nn.sigmoid(a)
            swish = a * sigma
            both = swish * b
            cols = pl.ds(at, TILE)
            p2[rows, cols] = swish
            p3[rows, cols] = b * sigma * (1.0 + a * (1.0 - sigma))
            hid[rows, cols] = both.astype(jnp.bfloat16)
            return inner

        return lax.fori_loop(0, ROWS // CHUNK, rows_of, carry)

    lax.fori_loop(0, hidden // TILE, forward_tile, 0)

    def reduce(a, q, r):
        n = a * PARTS + q
        rows = slice(STEP_AT[r], STEP_AT[r] + STEP_ROWS[r])
        return pltpu.make_async_remote_copy(
            src_ref=sb.at[n, rows, :],
            dst_ref=rb.at[n, rows, :],
            send_sem=rs_send.at[n * 4 + r],
            recv_sem=rs_recv.at[n * 4 + r],
            device_id=member(1 << ORDER[q][3 - r]),
            device_id_type=MESH,
        )

    def permuted(ref, q):
        return jnp.concatenate(
            [ref[SLOT[q][p] * TOK : (SLOT[q][p] + 1) * TOK, :] for p in range(MEMBERS)], axis=0
        )

    def produce(a, q, ref, weight):
        n = a * PARTS + q
        tile = min(TILE, part)
        for c in range(part // tile):
            cols = slice(c * tile, (c + 1) * tile)
            rows = slice(q * part + c * tile, q * part + (c + 1) * tile)
            value = nt_dot(permuted(ref, q), weight[rows, :])
            sb[n, 0:HALF, cols] = value[HALF:, :].astype(jnp.bfloat16)
            acc[n, :, cols] = value[:HALF, :]
        reduce(a, q, 0).start()

    for copy in weights[4:]:
        copy.wait()
    for q in range(PARTS):
        produce(0, q, hid, dn_v)

    for q in range(PARTS):
        gather(1, q, 3).wait_recv()
    ggacc[...] = jnp.zeros_like(ggacc)

    def backward_tile(n, carry):
        at = pl.multiple_of(n * TILE, TILE)
        up_at = pl.multiple_of(hidden + n * TILE, TILE)
        total = jnp.zeros((ROWS, TILE), jnp.float32)
        for q in range(PARTS):
            total += nn_dot(block(1, q), dn_v[q * part : (q + 1) * part, pl.ds(at, TILE)])
        ta[...] = total

        def rows_of(i, inner):
            rows = pl.ds(pl.multiple_of(i * CHUNK, CHUNK), CHUNK)
            cols = pl.ds(at, TILE)
            back = ta[rows, :]
            terms = back * hid[rows, cols].astype(jnp.float32)
            ggacc[rows, :] += terms[:, :LANES] + terms[:, LANES:]
            dpre[rows, cols] = (back * p3[rows, cols]).astype(jnp.bfloat16)
            dpre[rows, pl.ds(up_at, TILE)] = (back * p2[rows, cols]).astype(jnp.bfloat16)
            return inner

        return lax.fori_loop(0, ROWS // CHUNK, rows_of, carry)

    lax.fori_loop(0, hidden // TILE, backward_tile, 0)

    for q in range(PARTS):
        produce(1, q, dpre, gu_v)

    def spread(row):
        row = jnp.broadcast_to(row, (TOK, LANES))
        column = jnp.sum(jnp.where(lane == sub, row, 0.0), axis=1, keepdims=True)
        return jnp.broadcast_to(column, (TOK, LANES))

    for j in range(MEMBERS):
        rows = slice(j * TOK, (j + 1) * TOK)
        gcol[rows, :] = spread(gpos[j : j + 1, :])
        pcol[rows, :] = spread(gpos[MEMBERS + j : MEMBERS + j + 1, :])
        column = jnp.sum(ggacc[rows, :], axis=1, keepdims=True)
        qrow[j : j + 1, :] = jnp.sum(jnp.where(lane == sub, column, 0.0), axis=0, keepdims=True)
    for i in range(4):
        near_to[i].wait_recv()
        for j in range(MEMBERS):
            rows = slice(j * TOK, (j + 1) * TOK)
            other = j ^ (1 << i)
            if j >> i & 1:
                gnear[i, rows, :] = jnp.zeros((TOK, LANES), jnp.float32)
                pnear[i, rows, :] = jnp.zeros((TOK, LANES), jnp.float32)
            else:
                gnear[i, rows, :] = spread(knear[i, other : other + 1, :])
                pnear[i, rows, :] = spread(knear[i, MEMBERS + other : MEMBERS + other + 1, :])

    for b in range(levels):

        @pl.when(bit(b) == 0)
        def _():
            pl.semaphore_wait(ready.at[b], 1)
            spare_to[b].start()

    limit = cap
    for b in range(levels):
        spare_to[b].wait_recv()
        limit += drecv[b] * (mask_s[...] == 1 << b).astype(jnp.float32)
    lsend[0] = limit
    limits_to = [near(lsend.at[0], lnear.at[i], l_send, l_recv, i) for i in range(4)]
    for copy in limits_to:
        copy.start()
    gcol[...] = jnp.where(pcol[...] < limit, gcol[...], 0.0)
    kept = (mat > 0.0) & (position < limit)
    gkeep[...] = jnp.where(kept, qrow[...], 0.0)
    for j in range(MEMBERS):
        qsend[j] = gkeep[j : j + 1, :]
    for copy in quot_to:
        copy.start()
    for i in range(4):
        limits_to[i].wait_recv()
        gnear[i] = jnp.where(pnear[i] < lnear[i], gnear[i], 0.0)

    def widen(rows):
        return jnp.concatenate([jnp.concatenate(rows, axis=0)] * (part // LANES), axis=1)

    def gate_rows(q, first, count):
        slots_in = [SLOT[q][p] * TOK for p in range(first, first + count)]
        return widen([gcol[at : at + TOK, :] for at in slots_in])

    def near_rows(q, first, count):
        slots_in = [SLOT[q][p] * TOK for p in range(first, first + count)]
        return widen([gnear[ORDER[q][3], at : at + TOK, :] for at in slots_in])

    def total_of(n, q, first, count, steps):
        size = count * TOK
        at = first * TOK
        total = acc[n, at : at + size, :] * gate_rows(q, first, count)
        for i in range(steps):
            term = rb[n, STEP_AT[i] + at : STEP_AT[i] + at + size, :].astype(jnp.float32)
            total += term * near_rows(q, first, count) if i == 0 else term
        return total.astype(jnp.bfloat16)

    def pass_on(a, q, r):
        n = a * PARTS + q
        reduce(a, q, r - 1).wait_recv()
        size = STEP_ROWS[r]
        count = size // TOK
        sb[n, STEP_AT[r] : STEP_AT[r] + size, :] = total_of(n, q, count, count, r)
        reduce(a, q, r).start()

    def finish(a, q, ref):
        n = a * PARTS + q
        reduce(a, q, 3).wait_recv()
        ref[:, q * part : (q + 1) * part] = total_of(n, q, 0, 1, 4)

    for q in range(PARTS):
        pass_on(0, q, 1)
    for q in range(PARTS):
        pass_on(1, q, 1)

    for r in range(2, 4):
        for q in range(PARTS):
            pass_on(0, q, r)
        for q in range(PARTS):
            pass_on(1, q, r)

    gmat[0:1, :] = qsend[0]
    for j in range(1, MEMBERS):
        quot_to[j - 1].wait_recv()
        gmat[j : j + 1, :] = qrecv[j]
    by_slot = gmat[:, 0:TOK]
    for k in range(TOPK):
        ggrad_ref[k : k + 1, :] = jnp.sum(
            jnp.where(slots == rel[k : k + 1, :], by_slot, 0.0), axis=0, keepdims=True
        )

    for q in range(PARTS):
        finish(0, q, out_ref)
    for q in range(PARTS):
        finish(1, q, igrad_ref)

    for a in range(2):
        for q in range(PARTS):
            for s in range(4):
                gather(a, q, s).wait_send()
                reduce(a, q, s).wait_send()
    for copy in gates_to + spare_to + quot_to + near_to + limits_to:
        copy.wait_send()


def body(tokens, grad_out, gate_probs, routes, capacity, pair_mask, gate_up_weight, down_weight):
    width = tokens.shape[1]
    hidden = down_weight.shape[2]
    part = width // PARTS
    levels = lax.axis_size("dp").bit_length() - 1
    vmem = pl.BlockSpec(memory_space=pltpu.VMEM)
    in_hbm = pl.BlockSpec(memory_space=pltpu.HBM)
    f32, b16 = jnp.float32, jnp.bfloat16
    dma = pltpu.SemaphoreType.DMA
    streams = 2 * PARTS
    out, igrad, ggrad = pl.pallas_call(
        functools.partial(kernel, levels),
        out_shape=(
            jax.ShapeDtypeStruct((TOK, width), b16),
            jax.ShapeDtypeStruct((TOK, width), b16),
            jax.ShapeDtypeStruct((TOPK, TOK), f32),
        ),
        in_specs=[in_hbm] * 8,
        out_specs=(vmem, vmem, vmem),
        scratch_shapes=[
            pltpu.VMEM((width, 2 * hidden), b16),
            pltpu.VMEM((width, hidden), b16),
            pltpu.VMEM((streams, ROWS, part), b16),
            pltpu.VMEM((streams, 240, part), b16),
            pltpu.VMEM((streams, 240, part), b16),
            pltpu.VMEM((streams, HALF, part), f32),
            pltpu.VMEM((ROWS, hidden), f32),
            pltpu.VMEM((ROWS, hidden), f32),
            pltpu.VMEM((ROWS, hidden), b16),
            pltpu.VMEM((ROWS, 2 * hidden), b16),
            pltpu.VMEM((ROWS, TILE), f32),
            pltpu.VMEM((ROWS, TILE), f32),
            pltpu.VMEM((TOPK, TOK), b16),
            pltpu.VMEM((TOPK, TOK), jnp.int32),
            pltpu.VMEM((1, 1), jnp.int32),
            pltpu.VMEM((1, 1), jnp.int32),
            pltpu.VMEM((MEMBERS, 1, LANES), f32),
            pltpu.VMEM((MEMBERS, 1, LANES), f32),
            pltpu.VMEM((MEMBERS, LANES), f32),
            pltpu.VMEM((MEMBERS, LANES), f32),
            pltpu.VMEM((2 * MEMBERS, LANES), f32),
            pltpu.VMEM((4, 2 * MEMBERS, LANES), f32),
            pltpu.VMEM((ROWS, LANES), f32),
            pltpu.VMEM((4, ROWS, LANES), f32),
            pltpu.VMEM((ROWS, LANES), f32),
            pltpu.VMEM((4, ROWS, LANES), f32),
            pltpu.VMEM((1, 1, LANES), f32),
            pltpu.VMEM((4, 1, LANES), f32),
            pltpu.VMEM((MEMBERS, LANES), f32),
            pltpu.VMEM((ROWS, LANES), f32),
            pltpu.VMEM((MEMBERS, 1, LANES), f32),
            pltpu.VMEM((MEMBERS, 1, LANES), f32),
            pltpu.VMEM((1, 1, LANES), f32),
            pltpu.VMEM((16, 1, LANES), f32),
            dma((streams,)),
            dma((4,)),
            dma((8,)),
            dma((streams * 4,)),
            dma((streams * 4,)),
            dma((streams * 4,)),
            dma((streams * 4,)),
            dma((MEMBERS,)),
            dma((MEMBERS,)),
            dma((MEMBERS,)),
            dma((MEMBERS,)),
            dma((16,)),
            dma((16,)),
            dma((4,)),
            dma((4,)),
            dma((4,)),
            dma((4,)),
            pltpu.SemaphoreType.REGULAR((max(levels, 1),)),
        ],
        compiler_params=pltpu.CompilerParams(
            collective_id=0, has_side_effects=True, vmem_limit_bytes=60 * 1024 * 1024
        ),
        cost_estimate=pl.CostEstimate(
            flops=2 * ROWS * width * hidden * 6,
            bytes_accessed=width * hidden * 6,
            transcendentals=ROWS * hidden,
        ),
    )(
        tokens,
        grad_out,
        gate_probs.T,
        routes.T,
        capacity,
        pair_mask.reshape(1, 1),
        gate_up_weight,
        down_weight,
    )
    return (out, igrad, ggrad.T)


def solution(mesh):
    rows = P(("dp", "expert"), None)
    return jax.shard_map(
        body,
        mesh=mesh,
        in_specs=(
            rows,
            rows,
            rows,
            rows,
            P("dp", "expert"),
            P("expert"),
            P("expert", None, None),
            P("expert", None, None),
        ),
        out_specs=(rows, rows, rows),
        check_vma=False,
    )
```
